128 devices in a mesh: ctx: 16 (over y_lo, x, core), head: 8 (over y_hi, z).
Axes of the slice: x: 4, y: 4 (y_hi: 2, y_lo: 2; y = y_hi * 2 + y_lo), z: 4, core: 2. Of those that a mesh axis runs over, the one named last changes fastest.
Arguments:
- queries: bfloat16 [4096, 8192], P('ctx', 'head'), may hold values from -5 to 5
- keys: bfloat16 [4096, 1024], P('ctx', 'head'), may hold values from -5 to 5
- values: bfloat16 [4096, 1024], P('ctx', 'head'), may hold values from -5 to 5
- gate_logit: bfloat16 [4096, 8], P('ctx', 'head'), may hold values from -4 to 2
- out_grad: bfloat16 [4096, 8192], P('ctx', 'head'), may hold values from -5 to 5
- stretch_place: int32 [32], replicated, may hold values from 0 to 31, as said below
Outputs:
- query_grad: bfloat16 [4096, 8192], P('ctx', 'head')
- key_grad: bfloat16 [4096, 1024], P('ctx', 'head')
- value_grad: bfloat16 [4096, 1024], P('ctx', 'head')
- gate_grad: float32 [4096, 8], P('ctx', 'head')
The draws below stay inside these ranges and needn't reach their ends.
Inputs may be any that keep to these rules, and one draw needn't show every extreme that they name: `stretch_place`: entries 2d and 2d + 1 are the spans stored on index d of ctx; they sum to 31, and every span appears once.
All inputs are finite; a program needn't handle non-finite values.
Results may differ from the reference program's by a relative error of at most 0.025.
Values may be sent and summed in bfloat16 or wider, within the bound.
A program may use at most 64 MiB of HBM per device.

```python
import jax
import jax.numpy as jnp
from jax import lax

HQ = 64
KVH = 8
DH = 128
GROUP = 8
TOK_DEV = 256
SPAN = 128
TOKENS = 4096
BLOCKS = 32
DELAY = 256


def draw_queries(key, part):
    key = jax.random.fold_in(key, 11)
    first_key = jax.random.fold_in(key, 0)
    return jnp.clip(jax.random.normal(first_key, (TOKENS, HQ * DH), jnp.float32), -5.0, 5.0).astype(jnp.bfloat16)


def draw_keys(key, part):
    key = jax.random.fold_in(key, 23)
    first_key = jax.random.fold_in(key, 0)
    return jnp.clip(jax.random.normal(first_key, (TOKENS, KVH * DH), jnp.float32), -5.0, 5.0).astype(jnp.bfloat16)


def draw_stretch_place(key, part):
    key = jax.random.fold_in(key, 29)
    first_key, second_key = jax.random.split(key)
    half_count = BLOCKS // 2
    low_spans = jax.random.permutation(first_key, half_count).astype(jnp.int32)
    flipped = jax.random.randint(second_key, (half_count,), 0, 2, dtype=jnp.int32)
    high_spans = BLOCKS - 1 - low_spans
    first_slot = jnp.where(flipped == 1, high_spans, low_spans)
    second_slot = jnp.where(flipped == 1, low_spans, high_spans)
    return jnp.stack([first_slot, second_slot], axis=1).reshape(BLOCKS).astype(jnp.int32)


def block_scale(stream_key, shape, cuts, least, high):
    gain, own = 1.0, jax.random.fold_in(stream_key, 6)
    for dim, shards_of in cuts:
        draws = jnp.exp(jax.random.uniform(jax.random.fold_in(own, dim), (shards_of,), jnp.float32, least / len(cuts), high / len(cuts)))
        gain = gain * jnp.repeat(draws, shape[dim] // shards_of).reshape([-1 if axis == dim else 1 for axis in range(len(shape))])
    return gain


def gaussian(rng, dims, spread, bound, shards=(), kind=jnp.bfloat16):
    array = spread * jax.random.normal(rng, dims, jnp.float32)
    if shards:
        array = array * block_scale(rng, dims, shards, -0.22, 0.18)
    return jnp.clip(array, -bound, bound).astype(kind)


def setup_inputs(seed: int = 0) -> dict:
    key_list = jax.random.split(jax.random.key(seed), 7)
    return {
        "queries": draw_queries(jax.random.fold_in(key_list[6], 71), 0),
        "keys": draw_keys(jax.random.fold_in(key_list[6], 71), 0),
        "values": gaussian(key_list[2], (TOKENS, KVH * DH), 1.0, 5.0, ((0, 16), (1, 8))),
        "gate_logit": jnp.clip(-4.0 + 6.0 * jax.random.uniform(key_list[3], (TOKENS, KVH), jnp.float32) ** block_scale(key_list[3], (TOKENS, KVH), ((0, 16), (1, 8)), -0.2, 0.2), -4.0, 2.0).astype(jnp.bfloat16),
        "out_grad": gaussian(key_list[4], (TOKENS, HQ * DH), 1.0, 5.0, ((0, 16), (1, 8))),
        "stretch_place": draw_stretch_place(jax.random.fold_in(key_list[6], 71), 0),
    }


NEG_FILL = -1e30


def stored_positions(stretch_place, total_rows, span_rows):
    offsets = jnp.arange(total_rows, dtype=jnp.int32) % span_rows
    span_ids = jnp.repeat(stretch_place.astype(jnp.int32), span_rows, total_repeat_length=total_rows)
    return span_ids * span_rows + offsets


def reference(queries, keys, values, gate_logit, out_grad, stretch_place):
    score_scale = DH ** -0.5
    positions = stored_positions(stretch_place, TOKENS, SPAN)
    gate_values = gate_logit.astype(jnp.float32)
    evict_bias = jax.nn.log_sigmoid(-gate_values).T
    keep_prob = jax.nn.sigmoid(gate_values)
    blocks = TOKENS // TOK_DEV
    query_heads = queries.astype(jnp.float32).reshape(blocks, TOK_DEV, KVH, GROUP, DH).transpose(2, 0, 1, 3, 4)
    grad_heads = out_grad.astype(jnp.float32).reshape(blocks, TOK_DEV, KVH, GROUP, DH).transpose(2, 0, 1, 3, 4)
    key_heads = keys.astype(jnp.float32).reshape(TOKENS, KVH, DH).transpose(1, 0, 2)
    value_heads = values.astype(jnp.float32).reshape(TOKENS, KVH, DH).transpose(1, 0, 2)
    query_pos = positions.reshape(blocks, TOK_DEV)

    def one_head(inputs):
        query_blocks, grad_blocks, key_rows, value_rows, bias_row = inputs

        def per_block(grad_sums, block_in):
            query_block, grad_block, pos_block = block_in
            scores = jnp.einsum("qgd,td->gqt", query_block, key_rows) * score_scale
            offset = pos_block[:, None] - positions[None, :]
            scores = scores + jnp.where(offset >= DELAY, bias_row[None, :], 0.0)[None]
            live_mask = (offset >= 0)[None]
            scores = jnp.where(live_mask, scores, NEG_FILL)
            row_max = jnp.max(scores, axis=-1, keepdims=True)
            log_total = row_max + jnp.log(jnp.sum(jnp.exp(scores - row_max), axis=-1, keepdims=True))
            attn_prob = jnp.where(live_mask, jnp.exp(scores - log_total), 0.0)
            output = jnp.einsum("gqt,td->qgd", attn_prob, value_rows, precision=lax.Precision.HIGHEST)
            delta_row = jnp.sum(grad_block * output, axis=-1).T
            prob_grad = jnp.einsum("qgd,td->gqt", grad_block, value_rows)
            score_grad = attn_prob * (prob_grad - delta_row[:, :, None])
            grad_low = lax.optimization_barrier(score_grad.astype(jnp.bfloat16)).astype(jnp.float32)
            prob_low = lax.optimization_barrier(attn_prob.astype(jnp.bfloat16)).astype(jnp.float32)
            query_part = jnp.einsum("gqt,td->qgd", grad_low, key_rows) * score_scale
            key_sum, value_sum, gate_sum = grad_sums
            key_sum = key_sum + jnp.einsum("gqt,qgd->td", grad_low, query_block) * score_scale
            value_sum = value_sum + jnp.einsum("gqt,qgd->td", prob_low, grad_block)
            gate_sum = gate_sum + jnp.sum(jnp.where((offset >= DELAY)[None], score_grad, 0.0), axis=(0, 1))
            return (key_sum, value_sum, gate_sum), query_part.astype(jnp.bfloat16)

        start_sums = (jnp.zeros((TOKENS, DH), jnp.float32), jnp.zeros((TOKENS, DH), jnp.float32), jnp.zeros((TOKENS,), jnp.float32))
        grad_sums, query_parts = lax.scan(per_block, start_sums, (query_blocks, grad_blocks, query_pos))
        return grad_sums[0], grad_sums[1], grad_sums[2], query_parts

    key_all, value_all, gate_all, query_all = lax.map(one_head, (query_heads, grad_heads, key_heads, value_heads, evict_bias))
    query_grad = query_all.transpose(1, 2, 0, 3, 4).reshape(TOKENS, HQ * DH)
    key_grad = key_all.transpose(1, 0, 2).reshape(TOKENS, KVH * DH).astype(jnp.bfloat16)
    value_grad = value_all.transpose(1, 0, 2).reshape(TOKENS, KVH * DH).astype(jnp.bfloat16)
    gate_grad = -keep_prob * gate_all.T
    return query_grad, key_grad, value_grad, gate_grad
```

```python
import functools

import jax
import jax.numpy as jnp
from jax import lax
from jax.experimental import pallas as pl
from jax.experimental.pallas import tpu as pltpu
from jax.sharding import PartitionSpec as P

DELAY = 256
SPAN = 128
HEADS = 8
WIDE = SPAN * HEADS
CHIPS = 8
STEPS = 17
ROWS = 528
NEG = -1e30
LOG2E = 1.4426950408889634
SCALE = 128 ** (-0.5)
MESH = pl.DeviceIdType.MESH
F32, BF16 = jnp.float32, jnp.bfloat16


def step_slot(s):
    half, odd = lax.div(s, 2), lax.rem(s, 2)
    first = lax.div(1, half + 1)
    return 2 * half - odd - lax.div(s, 16) + first * odd


def forward_step(i):
    half, odd = lax.div(i, 2), lax.rem(i, 2)
    second = lax.div(2, half + 1) - 2 * lax.div(1, half + 1)
    return i + second * (1 - 2 * odd)


def chip_at(y, x, j, sign):
    dy, dx = lax.div(j, 4), lax.rem(j, 4)
    return lax.rem(y + 2 + sign * dy, 2) * 4 + lax.rem(x + 4 + sign * dx, 4)


def kernel(
    place, q_ref, k_ref, v_ref, gate_ref, o_ref,
    dq_ref, dk_ref, dv_ref, dg_ref,
    blocks, qc, qct, oc, oct_, wt_all, e_all, p_all, stat, total, ds_all,
    cur, cur_gate, own, own_gate, pre_out, pre_in, sum_out, sum_in,
    own_send, fwd_send, block_recv, pre_send, pre_recv, sum_send, sum_recv,
):
    me = lax.axis_index("ctx")
    core = lax.rem(me, 2)
    chip = lax.div(me, 2)
    y, x = lax.div(chip, 4), lax.rem(chip, 4)
    partner = me + 1 - 2 * core

    barrier = pltpu.get_barrier_semaphore()
    pl.semaphore_signal(barrier, inc=1, device_id={"ctx": partner}, device_id_type=MESH)
    for j in range(1, CHIPS):
        other = chip_at(y, x, jnp.int32(j), 1) * 2 + core
        pl.semaphore_signal(barrier, inc=1, device_id={"ctx": other}, device_id_type=MESH)

    blocks[0, 0:256, :] = k_ref[...]
    blocks[0, 256:512, :] = v_ref[...]
    blocks[0, 512:528, :] = gate_ref[...]
    pl.semaphore_wait(barrier, CHIPS)

    def own_copy(j):
        if j == 0:
            target, slot = partner, 1
        else:
            target, slot = chip_at(y, x, jnp.int32(j), 1) * 2 + core, 2 * j
        return pltpu.make_async_remote_copy(
            src_ref=blocks.at[0], dst_ref=blocks.at[slot], send_sem=own_send.at[j],
            recv_sem=block_recv.at[slot], device_id={"ctx": target}, device_id_type=MESH)

    def forward_copy(j):
        return pltpu.make_async_remote_copy(
            src_ref=blocks.at[2 * j], dst_ref=blocks.at[2 * j + 1], send_sem=fwd_send.at[j],
            recv_sem=block_recv.at[2 * j + 1], device_id={"ctx": partner}, device_id_type=MESH)

    def pre_copy(j):
        return pltpu.make_async_remote_copy(
            src_ref=pre_out.at[j], dst_ref=pre_in.at[j], send_sem=pre_send.at[j],
            recv_sem=pre_recv.at[j], device_id={"ctx": partner}, device_id_type=MESH)

    def sum_copy(j):
        target = chip_at(y, x, j, -1) * 2 + core
        return pltpu.make_async_remote_copy(
            src_ref=sum_out.at[j], dst_ref=sum_in.at[j], send_sem=sum_send.at[j],
            recv_sem=sum_recv.at[j], device_id={"ctx": target}, device_id_type=MESH)

    for j in range(CHIPS):
        own_copy(j).start()

    for h in range(HEADS):
        wide = slice(h * SPAN, (h + 1) * SPAN)
        for q in range(2):
            part = slice(q * SPAN, (q + 1) * SPAN)
            for src, plain, turned in ((q_ref, qc, qct), (o_ref, oc, oct_)):
                tile = src[part, wide]
                plain[wide, part] = tile
                turned[part, wide] = tile.T

    key_row = lax.broadcasted_iota(jnp.int32, (SPAN, SPAN), 0)
    query_col = lax.broadcasted_iota(jnp.int32, (SPAN, SPAN), 1)
    lag = query_col - key_row
    a0, a1 = place[2 * me], place[2 * me + 1]
    a_low = jnp.minimum(a0, a1)
    q_high = (a1 > a0).astype(jnp.int32)

    def pairs(s):
        slot = step_slot(s)
        theirs = chip_at(y, x, lax.div(slot, 2), -1) * 2 + lax.rem(core + slot, 2)
        b0, b1 = place[2 * theirs], place[2 * theirs + 1]
        k_low = (b1 < b0).astype(jnp.int32)
        below = jnp.minimum(b0, b1) < a_low
        diag = s == 0
        cross = s == 1
        k0 = jnp.where(diag, 0, jnp.where(cross, k_low, jnp.where(below, k_low, 0)))
        k1 = jnp.where(diag, 1, jnp.where(cross, k_low, jnp.where(below, k_low, 1)))
        q0 = jnp.where(diag, 0, jnp.where(cross, q_high, jnp.where(below, 0, q_high)))
        q1 = jnp.where(diag, 1, jnp.where(cross, q_high, jnp.where(below, 1, q_high)))
        out = []
        for u, (k, q) in enumerate(((k0, q0), (k1, q1))):
            apart = jnp.where(q == 0, a0, a1) - jnp.where(k == 0, b0, b1)
            live = -SPAN * apart
            if u == 1:
                live = jnp.where(cross, 4 * SPAN, live)
            out.append((k, q, DELAY - SPAN * apart, live))
        return slot, out

    def take(first, a, b):
        return lax.select(first, a, b)

    def first_pass(i, _):
        s = forward_step(i)
        slot, units = pairs(s)

        @pl.when(s >= 2)
        def _():
            pltpu.make_async_remote_copy(
                src_ref=blocks.at[slot], dst_ref=blocks.at[slot], send_sem=own_send.at[0],
                recv_sem=block_recv.at[slot], device_id={"ctx": partner}, device_id_type=MESH).wait_recv()

            @pl.when(lax.rem(slot, 2) == 0)
            def _():
                forward_copy(lax.div(slot, 2)).start()

        k0, k1 = blocks[slot, 0:128, :].astype(F32), blocks[slot, 128:256, :].astype(F32)
        v0, v1 = blocks[slot, 256:384, :].astype(F32), blocks[slot, 384:512, :].astype(F32)
        gates = blocks[slot, 512:528, :].astype(F32)
        evict = -LOG2E * (jnp.maximum(gates, 0.0) + jnp.log(1.0 + jnp.exp(-jnp.abs(gates))))
        zero = jnp.zeros((SPAN, SPAN), F32)
        wk, wv, bias = [], [], []
        for u, (k, q, least, live) in enumerate(units):
            ku, vu = take(k == 0, k0, k1), take(k == 0, v0, v1)
            wk.append(jnp.concatenate([take(q == 0, ku, zero), take(q == 0, zero, ku)], axis=1).astype(BF16))
            wv.append(jnp.concatenate([take(q == 0, vu, zero), take(q == 0, zero, vu)], axis=1).astype(BF16))
            kt = ku.T
            columns = pl.ds(pl.multiple_of(s * 256 + u * SPAN, SPAN), SPAN)
            wt_all[0:128, columns] = take(q == 0, kt, zero).astype(BF16)
            wt_all[128:256, columns] = take(q == 0, zero, kt).astype(BF16)
            column = jnp.broadcast_to(take(k == 0, evict[0:1, :], evict[1:2, :]), (SPAN, SPAN)).T
            bias.append(jnp.where(lag >= live, jnp.where(lag >= least, column, 0.0), NEG))
        wk, wv = jnp.concatenate(wk, axis=0), jnp.concatenate(wv, axis=0)
        for c in range(4):
            cols = slice(c * 256, (c + 1) * 256)
            scores = jnp.dot(wk, qct[:, cols], preferred_element_type=F32)
            grads = jnp.dot(wv, oct_[:, cols], preferred_element_type=F32)
            for u in range(2):
                part = slice(u * SPAN, (u + 1) * SPAN)
                for h in range(2):
                    lane = slice(h * SPAN, (h + 1) * SPAN)
                    wide = slice(c * 256 + h * SPAN, c * 256 + (h + 1) * SPAN)
                    score = scores[part, lane] * (SCALE * LOG2E) + bias[u]
                    grad = grads[part, lane]
                    top = jnp.max(score, axis=0, keepdims=True)
                    e = jnp.exp2(score - top)
                    e_all[s, part, wide] = e
                    p_all[s, part, wide] = grad
                    stat[s, u:u + 1, wide] = top
                    stat[s, 2 + u:3 + u, wide] = jnp.sum(e, axis=0, keepdims=True)
                    stat[s, 4 + u:5 + u, wide] = jnp.sum(e * grad, axis=0, keepdims=True)
        return 0

    lax.fori_loop(0, STEPS, first_pass, 0)

    row = lax.broadcasted_iota(jnp.int32, (2, 1), 0)

    def combine(s, carry):
        top, mass, weighted = carry
        _, units = pairs(s)
        new = top
        for u, (_, q, _, _) in enumerate(units):
            new = jnp.maximum(new, jnp.where(row == q, stat[s, u:u + 1, :], NEG))
        keep = jnp.exp2(top - new)
        mass, weighted = mass * keep, weighted * keep
        for u, (_, q, _, _) in enumerate(units):
            factor = jnp.exp2(jnp.minimum(stat[s, u:u + 1, :] - new, 0.0))
            mass = mass + jnp.where(row == q, stat[s, 2 + u:3 + u, :] * factor, 0.0)
            weighted = weighted + jnp.where(row == q, stat[s, 4 + u:5 + u, :] * factor, 0.0)
        return new, mass, weighted

    start = (jnp.full((2, WIDE), NEG, F32), jnp.zeros((2, WIDE), F32), jnp.zeros((2, WIDE), F32))
    top, mass, weighted = lax.fori_loop(0, STEPS, combine, start)
    total[0:2, :] = top
    total[2:4, :] = 1.0 / mass
    total[4:6, :] = weighted / mass

    def pack(dst, key_part, value_part, gate_part):
        dst[0:256, :] = key_part.astype(BF16)
        dst[256:512, :] = value_part.astype(BF16)
        high = gate_part.astype(BF16).astype(F32)
        dst[512:528, :] = jnp.concatenate([high, gate_part - high], axis=0).astype(BF16)

    def unpack(src):
        tail = src[512:528, :].astype(F32)
        return src[0:256, :].astype(F32), src[256:512, :].astype(F32), tail[0:8] + tail[8:16]

    def second_pass(i, _):
        s = STEPS - 1 - i
        slot, units = pairs(s)
        j = lax.div(slot, 2)
        scale_rows, delta_rows = [], []
        for u, (_, q, _, _) in enumerate(units):
            first = q == 0
            peak = take(first, total[0:1, :], total[1:2, :])
            inverse = take(first, total[2:3, :], total[3:4, :])
            scale_rows.append(jnp.exp2(stat[s, u:u + 1, :] - peak) * inverse)
            delta_rows.append(take(first, total[4:5, :], total[5:6, :]))
        value_acc = jnp.zeros((256, 256), F32)
        key_acc = jnp.zeros((256, 256), F32)
        gate_acc = [jnp.zeros((SPAN, SPAN), F32), jnp.zeros((SPAN, SPAN), F32)]
        for c in range(4):
            cols = slice(c * 256, (c + 1) * 256)
            prob_rows, grad_rows = [], []
            for u in range(2):
                part = slice(u * SPAN, (u + 1) * SPAN)
                prob = e_all[s, part, cols] * scale_rows[u][:, cols]
                grad = prob * (p_all[s, part, cols] - delta_rows[u][:, cols])
                gate_acc[u] = gate_acc[u] + grad[:, 0:128] + grad[:, 128:256]
                prob_rows.append(prob.astype(BF16))
                grad_rows.append(grad.astype(BF16))
            prob_low = jnp.concatenate(prob_rows, axis=0)
            grad_low = jnp.concatenate(grad_rows, axis=0)
            ds_all[pl.ds(pl.multiple_of(s * 256, 256), 256), cols] = grad_low
            value_acc = value_acc + jnp.dot(prob_low, oc[cols, :], preferred_element_type=F32)
            key_acc = key_acc + jnp.dot(grad_low, qc[cols, :], preferred_element_type=F32)
        zero = jnp.zeros((SPAN, SPAN), F32)
        key_out, value_out = [zero, zero], [zero, zero]
        gate_out = [jnp.zeros((1, SPAN), F32), jnp.zeros((1, SPAN), F32)]
        for u, (k, q, least, _) in enumerate(units):
            part = slice(u * SPAN, (u + 1) * SPAN)
            key_u = take(q == 0, key_acc[part, 0:128], key_acc[part, 128:256]) * SCALE
            value_u = take(q == 0, value_acc[part, 0:128], value_acc[part, 128:256])
            gate_u = jnp.sum(jnp.where(lag >= least, gate_acc[u], 0.0).T, axis=0, keepdims=True)
            for half in range(2):
                hit = k == half
                key_out[half] = key_out[half] + take(hit, key_u, zero)
                value_out[half] = value_out[half] + take(hit, value_u, zero)
                gate_out[half] = gate_out[half] + take(hit, gate_u, jnp.zeros((1, SPAN), F32))
        cur[0:128, :] = key_out[0]
        cur[128:256, :] = key_out[1]
        cur[256:384, :] = value_out[0]
        cur[384:512, :] = value_out[1]
        cur_gate[...] = jnp.concatenate(gate_out + [jnp.zeros((6, SPAN), F32)], axis=0)

        @pl.when(lax.rem(slot, 2) == 1)
        def _():
            pack(pre_out.at[j], cur[0:256, :], cur[256:512, :], cur_gate[...])
            pre_copy(j).start()

        @pl.when(jnp.logical_and(lax.rem(slot, 2) == 0, s >= 2))
        def _():
            pre_copy(j).wait_recv()
            more = unpack(pre_in.at[j])
            pack(sum_out.at[j], cur[0:256, :] + more[0], cur[256:512, :] + more[1], cur_gate[...] + more[2])
            sum_copy(j).start()

        @pl.when(s == 1)
        def _():
            own[...] = cur[...]
            own_gate[...] = cur_gate[...]

        @pl.when(s == 0)
        def _():
            own[...] = own[...] + cur[...]
            own_gate[...] = own_gate[...] + cur_gate[...]

        return 0

    lax.fori_loop(0, STEPS, second_pass, 0)

    def query_pass(c, _):
        cols = pl.ds(pl.multiple_of(c * 256, 256), 256)
        acc = jnp.dot(wt_all[...], ds_all[:, cols], preferred_element_type=F32) * SCALE
        for q in range(2):
            for h in range(2):
                tile = acc[q * SPAN:(q + 1) * SPAN, h * SPAN:(h + 1) * SPAN].T
                lanes = pl.ds(pl.multiple_of(c * 256 + h * SPAN, SPAN), SPAN)
                dq_ref[q * SPAN:(q + 1) * SPAN, lanes] = tile.astype(BF16)
        return 0

    lax.fori_loop(0, 4, query_pass, 0)

    def collect(ref):
        key_part, value_part, gate_part = unpack(ref)
        own[0:256, :] = own[0:256, :] + key_part
        own[256:512, :] = own[256:512, :] + value_part
        own_gate[...] = own_gate[...] + gate_part

    pre_copy(0).wait_recv()
    collect(pre_in.at[0])

    def receive(i, _):
        j = CHIPS - 1 - i
        sum_copy(j).wait_recv()
        collect(sum_in.at[j])
        return 0

    lax.fori_loop(0, CHIPS - 1, receive, 0)
    dk_ref[...] = own[0:256, :].astype(BF16)
    dv_ref[...] = own[256:512, :].astype(BF16)
    gates = gate_ref[0:8, :].astype(F32)
    dg_ref[...] = -own_gate[...] / (1.0 + jnp.exp(-gates))

    for j in range(CHIPS):
        own_copy(j).wait_send()
        pre_copy(j).wait_send()
    for j in range(1, CHIPS):
        forward_copy(j).wait_send()
        sum_copy(jnp.int32(j)).wait_send()


def on_device(queries, keys, values, gate_logit, out_grad, stretch_place):
    rows = 2 * SPAN
    gates = jnp.pad(gate_logit.reshape(2, SPAN), ((0, 14), (0, 0)))
    vmem = pl.BlockSpec(memory_space=pltpu.VMEM)
    dma = pltpu.SemaphoreType.DMA
    dq, dk, dv, dg = pl.pallas_call(
        kernel,
        out_shape=(
            jax.ShapeDtypeStruct((rows, WIDE), BF16),
            jax.ShapeDtypeStruct((rows, SPAN), BF16),
            jax.ShapeDtypeStruct((rows, SPAN), BF16),
            jax.ShapeDtypeStruct((8, SPAN), F32),
        ),
        in_specs=[pl.BlockSpec(memory_space=pltpu.SMEM)] + [vmem] * 5,
        out_specs=(vmem,) * 4,
        scratch_shapes=[
            pltpu.VMEM((2 * CHIPS, ROWS, SPAN), BF16),
            pltpu.VMEM((WIDE, rows), BF16),
            pltpu.VMEM((rows, WIDE), BF16),
            pltpu.VMEM((WIDE, rows), BF16),
            pltpu.VMEM((rows, WIDE), BF16),
            pltpu.VMEM((rows, STEPS * rows), BF16),
            pltpu.VMEM((STEPS, rows, WIDE), F32),
            pltpu.VMEM((STEPS, rows, WIDE), F32),
            pltpu.VMEM((STEPS, 8, WIDE), F32),
            pltpu.VMEM((8, WIDE), F32),
            pltpu.VMEM((STEPS * rows, WIDE), BF16),
            pltpu.VMEM((2 * rows, SPAN), F32),
            pltpu.VMEM((8, SPAN), F32),
            pltpu.VMEM((2 * rows, SPAN), F32),
            pltpu.VMEM((8, SPAN), F32),
            pltpu.VMEM((CHIPS, ROWS, SPAN), BF16),
            pltpu.VMEM((CHIPS, ROWS, SPAN), BF16),
            pltpu.VMEM((CHIPS, ROWS, SPAN), BF16),
            pltpu.VMEM((CHIPS, ROWS, SPAN), BF16),
            dma((CHIPS,)), dma((CHIPS,)), dma((2 * CHIPS,)),
            dma((CHIPS,)), dma((CHIPS,)), dma((CHIPS,)), dma((CHIPS,)),
        ],
        compiler_params=pltpu.CompilerParams(
            collective_id=0, has_side_effects=True, vmem_limit_bytes=62 * 1024 * 1024),
    )(stretch_place, queries, keys, values, gates, out_grad)
    return dq, dk, dv, dg[:2].reshape(rows, 1)


def solution(mesh):
    whole = P("ctx", "head")
    return jax.shard_map(
        on_device, mesh=mesh, in_specs=(whole,) * 5 + (P(),), out_specs=(whole,) * 4, check_vma=False)
```

```python
import functools

import jax
import jax.numpy as jnp
from jax import lax
from jax.experimental import pallas as pl
from jax.experimental.pallas import tpu as pltpu
from jax.sharding import PartitionSpec as P

DELAY = 256
SPAN = 128
HEADS = 8
WIDE = SPAN * HEADS
CHIPS = 8
STEPS = 17
ROWS = 528
NEG = -1e30
LOG2E = 1.4426950408889634
SCALE = 128 ** (-0.5)
MESH = pl.DeviceIdType.MESH
F32, BF16 = jnp.float32, jnp.bfloat16


FIRST = (0, 1, 2, 3, 7, 9, 4, 8, 10, 5, 6, 11, 15, 12, 16, 13, 14)
SECOND = (14, 12, 13, 16, 11, 6, 15, 10, 5, 4, 9, 8, 3, 2, 7, 1, 0)
KEY, VALUE = pl.ds(0, 256), pl.ds(256, 272)
PARTS = (KEY, VALUE)


def table(values, i):
    out = i * 0 + values[0]
    for at, value in enumerate(values[1:], 1):
        out = jnp.where(i == at, value, out)
    return out


def chip_at(y, x, j, sign):
    dy, dx = (j // 4, j % 4) if isinstance(j, int) else (lax.div(j, 4), lax.rem(j, 4))
    return lax.rem(y + 2 + sign * dy, 2) * 4 + lax.rem(x + 4 + sign * dx, 4)


def kernel(
    place, q_ref, k_ref, v_ref, gate_ref, o_ref,
    dq_ref, dk_ref, dv_ref, dg_ref,
    blocks, q_in, o_in, qc, qct, oc, oct_, wt_all, e_all, p_all, stat, total, ds_all,
    cur, cur_gate, own, own_gate, held, held_gate, pre_out, pre_in, sum_out, sum_in,
    dq_out, dk_out, dv_out, dg_out,
    in_sem, out_sem, block_send, block_recv, pre_send, pre_recv, sum_send, sum_recv,
):
    me = lax.axis_index("ctx")
    core = lax.rem(me, 2)
    chip = lax.div(me, 2)
    y, x = lax.div(chip, 4), lax.rem(chip, 4)
    partner = me + 1 - 2 * core
    right = chip_at(y, x, 1, 1) * 2 + core
    left = chip_at(y, x, 1, -1) * 2 + core
    across = chip_at(y, x, 4, 1) * 2 + core

    barrier = pltpu.get_barrier_semaphore()
    for other in (partner, right, left, across):
        pl.semaphore_signal(barrier, inc=1, device_id={"ctx": other}, device_id_type=MESH)

    loads = [
        pltpu.make_async_copy(k_ref, blocks.at[0, pl.ds(0, 256)], in_sem.at[0]),
        pltpu.make_async_copy(v_ref, blocks.at[0, pl.ds(256, 256)], in_sem.at[1]),
        pltpu.make_async_copy(q_ref, q_in, in_sem.at[2]),
        pltpu.make_async_copy(o_ref, o_in, in_sem.at[3]),
    ]
    for load in loads:
        load.start()
    gate_row = gate_ref[...].astype(F32)
    blocks[0, 512:528, :] = jnp.concatenate(
        [gate_row[:, 0:128], gate_row[:, 128:256], jnp.zeros((14, SPAN), F32)], axis=0).astype(BF16)
    pl.semaphore_wait(barrier, 4)

    started = []

    def block_copy(source, slot, part, target, sem):
        return pltpu.make_async_remote_copy(
            src_ref=blocks.at[source, PARTS[part]], dst_ref=blocks.at[slot, PARTS[part]], send_sem=block_send.at[sem],
            recv_sem=block_recv.at[slot, part], device_id={"ctx": target}, device_id_type=MESH)

    def send(*what):
        started.append(what)
        block_copy(*what).start()

    def arrive(slot, part):
        pltpu.make_async_remote_copy(
            src_ref=blocks.at[slot, PARTS[part]], dst_ref=blocks.at[slot, PARTS[part]], send_sem=block_send.at[0],
            recv_sem=block_recv.at[slot, part], device_id={"ctx": partner}, device_id_type=MESH).wait_recv()

    def pass_on(slot, part):
        arrive(slot, part)
        send(slot, slot + 1, part, partner, 8 + slot + part)
        if (slot, part) == (2, 0):
            send(slot, 4, part, right, 24)
        if (slot, part) == (6, 1):
            send(slot, 4, part, left, 25)
        if slot == 8:
            send(slot, 10, part, right, 26 + part)
            send(slot, 14, part, left, 28 + part)
        if slot == 4:
            send(slot, 12, part, across, 30 + part)

    def pre_copy(j):
        return pltpu.make_async_remote_copy(
            src_ref=pre_out.at[j], dst_ref=pre_in.at[j], send_sem=pre_send.at[j],
            recv_sem=pre_recv.at[j], device_id={"ctx": partner}, device_id_type=MESH)

    def sum_copy(j, part):
        target = {1: left, 2: (left, right)[part], 3: right, 4: across, 5: left, 6: across, 7: right}[j]
        return pltpu.make_async_remote_copy(
            src_ref=sum_out.at[j, PARTS[part]], dst_ref=sum_in.at[j, PARTS[part]], send_sem=sum_send.at[j, part],
            recv_sem=sum_recv.at[j, part], device_id={"ctx": target}, device_id_type=MESH)

    for part in range(2):
        loads[part].wait()
        for at, (slot, target) in enumerate(((8, across), (2, right), (6, left), (1, partner))):
            send(0, slot, part, target, 2 * at + part)

    loads[2].wait()
    loads[3].wait()
    for h in range(HEADS):
        wide = slice(h * SPAN, (h + 1) * SPAN)
        for q in range(2):
            part = slice(q * SPAN, (q + 1) * SPAN)
            for src, plain, turned in ((q_in, qc, qct), (o_in, oc, oct_)):
                tile = src[part, wide]
                plain[wide, part] = tile
                turned[part, wide] = tile.T

    key_row = lax.broadcasted_iota(jnp.int32, (SPAN, SPAN), 0)
    query_col = lax.broadcasted_iota(jnp.int32, (SPAN, SPAN), 1)
    lag = query_col - key_row
    a0, a1 = place[2 * me], place[2 * me + 1]
    a_low = jnp.minimum(a0, a1)
    q_high = (a1 > a0).astype(jnp.int32)

    def pairs(s):
        slot = jnp.maximum(s - 1, 0)
        theirs = chip_at(y, x, lax.div(slot, 2), -1) * 2 + lax.rem(core + slot, 2)
        b0, b1 = place[2 * theirs], place[2 * theirs + 1]
        k_low = (b1 < b0).astype(jnp.int32)
        below = jnp.minimum(b0, b1) < a_low
        diag = s == 0
        cross = s == 1
        k0 = jnp.where(diag, 0, jnp.where(cross, k_low, jnp.where(below, k_low, 0)))
        k1 = jnp.where(diag, 1, jnp.where(cross, k_low, jnp.where(below, k_low, 1)))
        q0 = jnp.where(diag, 0, jnp.where(cross, q_high, jnp.where(below, 0, q_high)))
        q1 = jnp.where(diag, 1, jnp.where(cross, q_high, jnp.where(below, 1, q_high)))
        out = []
        for u, (k, q) in enumerate(((k0, q0), (k1, q1))):
            apart = jnp.where(q == 0, a0, a1) - jnp.where(k == 0, b0, b1)
            live = -SPAN * apart
            if u == 1:
                live = jnp.where(cross, 4 * SPAN, live)
            out.append((k, q, DELAY - SPAN * apart, live))
        return slot, out

    def take(first, a, b):
        return lax.select(first, a, b)

    def first_pass(i, _):
        s = table(FIRST, i)
        slot, units = pairs(s)

        @pl.when(i == 2)
        def _():
            arrive(1, 0)
            arrive(1, 1)

        @pl.when(i == 3)
        def _():
            for slot, part in ((2, 0), (8, 0), (6, 0), (6, 1), (8, 1), (2, 1)):
                pass_on(slot, part)

        @pl.when(i == 6)
        def _():
            pass_on(4, 0)

        @pl.when(i == 8)
        def _():
            pass_on(4, 1)

        @pl.when(i == 11)
        def _():
            for part in range(2):
                pass_on(10, part)
                pass_on(14, part)

        @pl.when(i == 14)
        def _():
            for part in range(2):
                pass_on(12, part)

        @pl.when(jnp.logical_and(i >= 6, lax.rem(slot, 2) == 1))
        def _():
            arrive(slot, 0)
            arrive(slot, 1)

        k0, k1 = blocks[slot, 0:128, :].astype(F32), blocks[slot, 128:256, :].astype(F32)
        v0, v1 = blocks[slot, 256:384, :].astype(F32), blocks[slot, 384:512, :].astype(F32)
        gates = blocks[slot, 512:528, :].astype(F32)
        evict = -LOG2E * (jnp.maximum(gates, 0.0) + jnp.log(1.0 + jnp.exp(-jnp.abs(gates))))
        zero = jnp.zeros((SPAN, SPAN), F32)
        wk, wv, bias = [], [], []
        for u, (k, q, least, live) in enumerate(units):
            ku, vu = take(k == 0, k0, k1), take(k == 0, v0, v1)
            wk.append(jnp.concatenate([take(q == 0, ku, zero), take(q == 0, zero, ku)], axis=1).astype(BF16))
            wv.append(jnp.concatenate([take(q == 0, vu, zero), take(q == 0, zero, vu)], axis=1).astype(BF16))
            kt = ku.T
            columns = pl.ds(pl.multiple_of(s * 256 + u * SPAN, SPAN), SPAN)
            wt_all[0:128, columns] = take(q == 0, kt, zero).astype(BF16)
            wt_all[128:256, columns] = take(q == 0, zero, kt).astype(BF16)
            column = jnp.broadcast_to(take(k == 0, evict[0:1, :], evict[1:2, :]), (SPAN, SPAN)).T
            bias.append(jnp.where(lag >= live, jnp.where(lag >= least, column, 0.0), NEG))
        wk, wv = jnp.concatenate(wk, axis=0), jnp.concatenate(wv, axis=0)
        for c in range(4):
            cols = slice(c * 256, (c + 1) * 256)
            scores = jnp.dot(wk, qct[:, cols], preferred_element_type=F32)
            grads = jnp.dot(wv, oct_[:, cols], preferred_element_type=F32)
            for u in range(2):
                part = slice(u * SPAN, (u + 1) * SPAN)
                for h in range(2):
                    lane = slice(h * SPAN, (h + 1) * SPAN)
                    wide = slice(c * 256 + h * SPAN, c * 256 + (h + 1) * SPAN)
                    score = scores[part, lane] * (SCALE * LOG2E) + bias[u]
                    grad = grads[part, lane]
                    top = jnp.max(score, axis=0, keepdims=True)
                    e = jnp.exp2(score - top)
                    e_all[s, part, wide] = e
                    p_all[s, part, wide] = grad
                    stat[s, u:u + 1, wide] = top
                    stat[s, 2 + u:3 + u, wide] = jnp.sum(e, axis=0, keepdims=True)
                    stat[s, 4 + u:5 + u, wide] = jnp.sum(e * grad, axis=0, keepdims=True)
        return 0

    lax.fori_loop(0, STEPS, first_pass, 0)

    row = lax.broadcasted_iota(jnp.int32, (2, 1), 0)

    def combine(s, carry):
        top, mass, weighted = carry
        _, units = pairs(s)
        new = top
        for u, (_, q, _, _) in enumerate(units):
            new = jnp.maximum(new, jnp.where(row == q, stat[s, u:u + 1, :], NEG))
        keep = jnp.exp2(top - new)
        mass, weighted = mass * keep, weighted * keep
        for u, (_, q, _, _) in enumerate(units):
            factor = jnp.exp2(jnp.minimum(stat[s, u:u + 1, :] - new, 0.0))
            mass = mass + jnp.where(row == q, stat[s, 2 + u:3 + u, :] * factor, 0.0)
            weighted = weighted + jnp.where(row == q, stat[s, 4 + u:5 + u, :] * factor, 0.0)
        return new, mass, weighted

    start = (jnp.full((2, WIDE), NEG, F32), jnp.zeros((2, WIDE), F32), jnp.zeros((2, WIDE), F32))
    top, mass, weighted = lax.fori_loop(0, STEPS, combine, start)
    total[0:2, :] = top
    total[2:4, :] = 1.0 / mass
    total[4:6, :] = weighted / mass

    def pack(dst, part, rows, gate_rows=None):
        if part == 0:
            dst[0:256, :] = rows.astype(BF16)
        else:
            dst[256:512, :] = rows.astype(BF16)
            high = gate_rows.astype(BF16).astype(F32)
            dst[512:528, :] = jnp.concatenate([high, gate_rows - high], axis=0).astype(BF16)

    def unpack_keys(src):
        return src[0:256, :].astype(F32)

    def unpack_values(src):
        tail = src[512:528, :].astype(F32)
        return src[256:512, :].astype(F32), tail[0:8] + tail[8:16]

    def leave(j, part, rows, gate_rows):
        if part == 0:
            pack(sum_out.at[j], 0, rows[0:256, :])
        else:
            pack(sum_out.at[j], 1, rows[256:512, :], gate_rows[...])
        sum_copy(j, part).start()

    def join(j, part, others):
        rows, gate_rows = held.at[j - 1], held_gate.at[j - 1]
        for other in others:
            sum_copy(other, part).wait_recv()
            add(rows, gate_rows, part, sum_in.at[other])
        leave(j, part, rows, gate_rows)

    def add(rows, gate_rows, part, src):
        if part == 0:
            rows[0:256, :] = rows[0:256, :] + unpack_keys(src)
        else:
            more, gate_more = unpack_values(src)
            rows[256:512, :] = rows[256:512, :] + more
            gate_rows[...] = gate_rows[...] + gate_more

    def second_pass(i, _):
        s = table(SECOND, i)
        slot, units = pairs(s)
        j = lax.div(slot, 2)
        scale_rows, delta_rows = [], []
        for u, (_, q, _, _) in enumerate(units):
            first = q == 0
            peak = take(first, total[0:1, :], total[1:2, :])
            inverse = take(first, total[2:3, :], total[3:4, :])
            scale_rows.append(jnp.exp2(stat[s, u:u + 1, :] - peak) * inverse)
            delta_rows.append(take(first, total[4:5, :], total[5:6, :]))
        value_acc = jnp.zeros((256, 256), F32)
        key_acc = jnp.zeros((256, 256), F32)
        gate_acc = [jnp.zeros((SPAN, SPAN), F32), jnp.zeros((SPAN, SPAN), F32)]
        for c in range(4):
            cols = slice(c * 256, (c + 1) * 256)
            prob_rows, grad_rows = [], []
            for u in range(2):
                part = slice(u * SPAN, (u + 1) * SPAN)
                prob = e_all[s, part, cols] * scale_rows[u][:, cols]
                grad = prob * (p_all[s, part, cols] - delta_rows[u][:, cols])
                gate_acc[u] = gate_acc[u] + grad[:, 0:128] + grad[:, 128:256]
                prob_rows.append(prob.astype(BF16))
                grad_rows.append(grad.astype(BF16))
            prob_low = jnp.concatenate(prob_rows, axis=0)
            grad_low = jnp.concatenate(grad_rows, axis=0)
            ds_all[pl.ds(pl.multiple_of(s * 256, 256), 256), cols] = grad_low
            value_acc = value_acc + jnp.dot(prob_low, oc[cols, :], preferred_element_type=F32)
            key_acc = key_acc + jnp.dot(grad_low, qc[cols, :], preferred_element_type=F32)
        zero = jnp.zeros((SPAN, SPAN), F32)
        key_out, value_out = [zero, zero], [zero, zero]
        gate_out = [jnp.zeros((1, SPAN), F32), jnp.zeros((1, SPAN), F32)]
        for u, (k, q, least, _) in enumerate(units):
            part = slice(u * SPAN, (u + 1) * SPAN)
            key_u = take(q == 0, key_acc[part, 0:128], key_acc[part, 128:256]) * SCALE
            value_u = take(q == 0, value_acc[part, 0:128], value_acc[part, 128:256])
            gate_u = jnp.sum(jnp.where(lag >= least, gate_acc[u], 0.0).T, axis=0, keepdims=True)
            for half in range(2):
                hit = k == half
                key_out[half] = key_out[half] + take(hit, key_u, zero)
                value_out[half] = value_out[half] + take(hit, value_u, zero)
                gate_out[half] = gate_out[half] + take(hit, gate_u, jnp.zeros((1, SPAN), F32))
        cur[0:128, :] = key_out[0]
        cur[128:256, :] = key_out[1]
        cur[256:384, :] = value_out[0]
        cur[384:512, :] = value_out[1]
        cur_gate[...] = jnp.concatenate(gate_out + [jnp.zeros((6, SPAN), F32)], axis=0)

        @pl.when(lax.rem(slot, 2) == 1)
        def _():
            pack(pre_out.at[j], 0, cur[0:256, :])
            pack(pre_out.at[j], 1, cur[256:512, :], cur_gate[...])
            pre_copy(j).start()

        @pl.when(jnp.logical_and(lax.rem(slot, 2) == 0, s >= 2))
        def _():
            pre_copy(j).wait_recv()
            cur[0:256, :] = cur[0:256, :] + unpack_keys(pre_in.at[j])
            more, gate_more = unpack_values(pre_in.at[j])
            cur[256:512, :] = cur[256:512, :] + more
            cur_gate[...] = cur_gate[...] + gate_more

        for at in range(1, CHIPS):
            @pl.when(s == 2 * at + 1)
            def _():
                for part in range(2):
                    if at in (5, 6, 7) or (at, part) in ((1, 1), (3, 0)):
                        leave(at, part, cur, cur_gate)
                if at in (1, 2, 3, 4):
                    held[at - 1] = cur[...]
                    held_gate[at - 1] = cur_gate[...]

        @pl.when(i == 10)
        def _():
            for part in range(2):
                join(2, part, (6,))

        @pl.when(i == 14)
        def _():
            for part in range(2):
                join(4, part, (5, 7))

        @pl.when(s == 1)
        def _():
            own[...] = cur[...]
            own_gate[...] = cur_gate[...]

        @pl.when(s == 0)
        def _():
            own[...] = own[...] + cur[...]
            own_gate[...] = own_gate[...] + cur_gate[...]

        return 0

    lax.fori_loop(0, STEPS, second_pass, 0)
    join(1, 0, (2,))
    join(3, 1, (2,))

    def query_pass(c, _):
        cols = pl.ds(pl.multiple_of(c * 256, 256), 256)
        acc = jnp.dot(wt_all[...], ds_all[:, cols], preferred_element_type=F32) * SCALE
        for q in range(2):
            for h in range(2):
                tile = acc[q * SPAN:(q + 1) * SPAN, h * SPAN:(h + 1) * SPAN].T
                lanes = pl.ds(pl.multiple_of(c * 256 + h * SPAN, SPAN), SPAN)
                dq_out[q * SPAN:(q + 1) * SPAN, lanes] = tile.astype(BF16)
        return 0

    lax.fori_loop(0, 4, query_pass, 0)

    stores = [
        pltpu.make_async_copy(dq_out, dq_ref, out_sem.at[0]),
        pltpu.make_async_copy(dk_out, dk_ref, out_sem.at[1]),
        pltpu.make_async_copy(dv_out, dv_ref, out_sem.at[2]),
        pltpu.make_async_copy(dg_out, dg_ref, out_sem.at[3]),
    ]
    stores[0].start()
    pre_copy(0).wait_recv()
    for part in range(2):
        add(own, own_gate, part, pre_in.at[0])
    for part in range(2):
        for j in (1, 3, 4):
            sum_copy(j, part).wait_recv()
            add(own, own_gate, part, sum_in.at[j])
        if part == 0:
            dk_out[...] = own[0:256, :].astype(BF16)
            stores[1].start()
    dv_out[...] = own[256:512, :].astype(BF16)
    gate_sum = jnp.concatenate([own_gate[0:1, :], own_gate[1:2, :]], axis=1)
    dg_out[...] = -gate_sum / (1.0 + jnp.exp(-gate_ref[...].astype(F32)))
    stores[2].start()
    stores[3].start()

    for what in started:
        block_copy(*what).wait_send()
    for j in range(CHIPS):
        pre_copy(j).wait_send()
    for j in range(1, CHIPS):
        for part in range(2):
            sum_copy(j, part).wait_send()
    for store in stores:
        store.wait()


def hand_over(*refs):
    sources, targets, held, sem_in, sem_out = refs[0:4], refs[4:8], refs[8:12], refs[12], refs[13]
    pulls = [pltpu.make_async_copy(sources[n], held[n], sem_in.at[n]) for n in range(4)]
    pushes = [pltpu.make_async_copy(held[n], targets[n], sem_out.at[n]) for n in range(4)]
    for pull in pulls:
        pull.start()
    for pull, push in zip(pulls, pushes):
        pull.wait()
        push.start()
    for push in pushes:
        push.wait()


def on_device(queries, keys, values, gate_logit, out_grad, stretch_place):
    rows = 2 * SPAN
    vmem = pl.BlockSpec(memory_space=pltpu.VMEM)
    anywhere = pl.BlockSpec(memory_space=pl.ANY)
    dma = pltpu.SemaphoreType.DMA
    outs = (
        jax.ShapeDtypeStruct((rows, WIDE), BF16),
        jax.ShapeDtypeStruct((rows, SPAN), BF16),
        jax.ShapeDtypeStruct((rows, SPAN), BF16),
        jax.ShapeDtypeStruct((1, rows), F32),
    )
    results = pl.pallas_call(
        kernel,
        out_shape=outs,
        in_specs=[pl.BlockSpec(memory_space=pltpu.SMEM), anywhere, anywhere, anywhere, vmem, anywhere],
        out_specs=(anywhere,) * 4,
        scratch_shapes=[
            pltpu.VMEM((2 * CHIPS, ROWS, SPAN), BF16),
            pltpu.VMEM((rows, WIDE), BF16),
            pltpu.VMEM((rows, WIDE), BF16),
            pltpu.VMEM((WIDE, rows), BF16),
            pltpu.VMEM((rows, WIDE), BF16),
            pltpu.VMEM((WIDE, rows), BF16),
            pltpu.VMEM((rows, WIDE), BF16),
            pltpu.VMEM((rows, STEPS * rows), BF16),
            pltpu.VMEM((STEPS, rows, WIDE), F32),
            pltpu.VMEM((STEPS, rows, WIDE), F32),
            pltpu.VMEM((STEPS, 8, WIDE), F32),
            pltpu.VMEM((8, WIDE), F32),
            pltpu.VMEM((STEPS * rows, WIDE), BF16),
            pltpu.VMEM((2 * rows, SPAN), F32),
            pltpu.VMEM((8, SPAN), F32),
            pltpu.VMEM((2 * rows, SPAN), F32),
            pltpu.VMEM((8, SPAN), F32),
            pltpu.VMEM((4, 2 * rows, SPAN), F32),
            pltpu.VMEM((4, 8, SPAN), F32),
            pltpu.VMEM((CHIPS, ROWS, SPAN), BF16),
            pltpu.VMEM((CHIPS, ROWS, SPAN), BF16),
            pltpu.VMEM((CHIPS, ROWS, SPAN), BF16),
            pltpu.VMEM((CHIPS, ROWS, SPAN), BF16),
            pltpu.VMEM((rows, WIDE), BF16),
            pltpu.VMEM((rows, SPAN), BF16),
            pltpu.VMEM((rows, SPAN), BF16),
            pltpu.VMEM((1, rows), F32),
            dma((4,)), dma((4,)), dma((32,)), dma((2 * CHIPS, 2)),
            dma((CHIPS,)), dma((CHIPS,)), dma((CHIPS, 2)), dma((CHIPS, 2)),
        ],
        compiler_params=pltpu.CompilerParams(
            collective_id=0, has_side_effects=True, vmem_limit_bytes=62 * 1024 * 1024),
    )(stretch_place, queries, keys, values, gate_logit.T, out_grad)
    dq, dk, dv, dg = pl.pallas_call(
        hand_over,
        out_shape=outs,
        in_specs=[anywhere] * 4,
        out_specs=(anywhere,) * 4,
        scratch_shapes=[pltpu.VMEM(out.shape, out.dtype) for out in outs] + [dma((4,)), dma((4,))],
        compiler_params=pltpu.CompilerParams(vmem_limit_bytes=62 * 1024 * 1024),
    )(*results)
    return dq, dk, dv, dg.T


def solution(mesh):
    whole = P("ctx", "head")
    return jax.shard_map(
        on_device, mesh=mesh, in_specs=(whole,) * 5 + (P(),), out_specs=(whole,) * 4, check_vma=False)
```

```python
import functools

import jax
import jax.numpy as jnp
from jax import lax
from jax.experimental import pallas as pl
from jax.experimental.pallas import tpu as pltpu
from jax.sharding import PartitionSpec as P

DELAY = 256
SPAN = 128
HEADS = 8
WIDE = SPAN * HEADS
CHIPS = 8
ROWS = 528
NEG = -1e30
LOG2E = 1.4426950408889634
SCALE = 128 ** (-0.5)
MESH = pl.DeviceIdType.MESH
F32, BF16 = jnp.float32, jnp.bfloat16


FIRST = ((0, 2, 8, 7, 4, 10, 11, 12), (1, 6, 3, 9, 5, 14, 15, 13))
SECOND = ((13, 12, 10, 14, 4, 8, 2, 6), (11, 15, 5, 9, 3, 7, 1, 0))
CROSS = 16
LATER = tuple(2 * (SECOND[0] if s in SECOND[0] else SECOND[1]).index(s) + (s in SECOND[1]) for s in range(CROSS))
PAIRS = 33
PARTS = (pl.ds(0, 256), pl.ds(256, 272))
QUARTERS = (pl.ds(0, 128), pl.ds(128, 128), pl.ds(256, 128), pl.ds(384, 144))


def table(values, i):
    out = i * 0 + values[0]
    for at, value in enumerate(values[1:], 1):
        out = jnp.where(i == at, value, out)
    return out


def chip_at(y, x, j, sign):
    dy, dx = (j // 4, j % 4) if isinstance(j, int) else (lax.div(j, 4), lax.rem(j, 4))
    return lax.rem(y + 2 + sign * dy, 2) * 4 + lax.rem(x + 4 + sign * dx, 4)


def kernel(
    place, q_ref, k_ref, v_ref, gate_ref, o_ref,
    dq_ref, dk_ref, dv_ref, dg_ref,
    blocks, qc, oc, wt_all, e_all, p_all, stat, total,
    cur, cur_gate, own, own_gate, held, held_gate, pre_out, pre_in, sum_out, sum_in,
    in_sem, block_send, block_recv, pre_send, pre_recv, sum_send, sum_recv,
):
    me = lax.axis_index("ctx")
    core = lax.rem(me, 2)
    chip = lax.div(me, 2)
    y, x = lax.div(chip, 4), lax.rem(chip, 4)
    partner = me + 1 - 2 * core
    right = chip_at(y, x, 1, 1) * 2 + core
    left = chip_at(y, x, 1, -1) * 2 + core
    across = chip_at(y, x, 4, 1) * 2 + core

    barrier = pltpu.get_barrier_semaphore()
    for other in (partner, right, left, across):
        pl.semaphore_signal(barrier, inc=1, device_id={"ctx": other}, device_id_type=MESH)

    def recv_sem(slot, part):
        return block_recv.at[16 + slot // 2 if part == 1 and slot in (2, 4, 6, 8) else slot]

    def send(source, slot, part, target):
        pltpu.make_async_remote_copy(
            src_ref=blocks.at[source, PARTS[part]], dst_ref=blocks.at[slot, PARTS[part]], send_sem=block_send,
            recv_sem=recv_sem(slot, part), device_id={"ctx": target}, device_id_type=MESH).start()

    def arrive(slot, part=None):
        where = blocks.at[slot] if part is None else blocks.at[slot, PARTS[part]]
        pltpu.make_async_remote_copy(
            src_ref=where, dst_ref=where, send_sem=block_send, recv_sem=recv_sem(slot, part or 0),
            device_id={"ctx": partner}, device_id_type=MESH).wait_recv()

    def pass_on(slot):
        for part in range(2):
            send(slot, slot + 1, part, partner)

    def pre_copy(j):
        return pltpu.make_async_remote_copy(
            src_ref=pre_out.at[j], dst_ref=pre_in.at[j], send_sem=pre_send,
            recv_sem=pre_recv.at[j], device_id={"ctx": partner}, device_id_type=MESH)

    def sum_copy(j, part):
        target = {1: left, 2: left if part < 2 else right, 3: right, 4: across, 5: left, 6: across, 7: right}[j]
        return pltpu.make_async_remote_copy(
            src_ref=sum_out.at[j - 1, QUARTERS[part]], dst_ref=sum_in.at[j - 1, QUARTERS[part]], send_sem=sum_send,
            recv_sem=sum_recv.at[j - 1, part], device_id={"ctx": target}, device_id_type=MESH)

    key_row = lax.broadcasted_iota(jnp.int32, (SPAN, SPAN), 0)
    query_col = lax.broadcasted_iota(jnp.int32, (SPAN, SPAN), 1)
    lag = query_col - key_row
    a0, a1 = place[2 * me], place[2 * me + 1]
    a_low = jnp.minimum(a0, a1)
    q_high = (a1 > a0).astype(jnp.int32)

    def block_of(slot):
        theirs = chip_at(y, x, lax.div(slot, 2), -1) * 2 + lax.rem(core + slot, 2)
        b0, b1 = place[2 * theirs], place[2 * theirs + 1]
        return b0, b1, (b1 < b0).astype(jnp.int32)

    def described(k, q, b0, b1):
        apart = jnp.where(q == 0, a0, a1) - jnp.where(k == 0, b0, b1)
        return k, q, DELAY - SPAN * apart, -SPAN * apart

    def pairs(s):
        b0, b1, k_low = block_of(s)
        below = jnp.minimum(b0, b1) < a_low
        diag = s == 0
        k0 = jnp.where(diag, 0, jnp.where(below, k_low, 0))
        k1 = jnp.where(diag, 1, jnp.where(below, k_low, 1))
        q0 = jnp.where(diag, 0, jnp.where(below, 0, q_high))
        q1 = jnp.where(diag, 1, jnp.where(below, 1, q_high))
        return described(k0, q0, b0, b1), described(k1, q1, b0, b1)

    def pair_across():
        b0, b1, k_low = block_of(core * 0)
        return (described(k_low, q_high, b0, b1),)

    def take(first, a, b):
        return lax.select(first, a, b)

    def scores_of(work, group):
        qct, oct_, raw_s, raw_g = work
        zero = jnp.zeros((SPAN, SPAN), F32)
        wk, wv, todo = [], [], []
        for s, slot, units in group:
            where = s if s is CROSS else table(LATER, s)
            k0, k1 = blocks[slot, 0:128, :].astype(F32), blocks[slot, 128:256, :].astype(F32)
            v0, v1 = blocks[slot, 256:384, :].astype(F32), blocks[slot, 384:512, :].astype(F32)
            gates = blocks[slot, 512:528, :].astype(F32)
            evict = -LOG2E * (jnp.maximum(gates, 0.0) + jnp.log(1.0 + jnp.exp(-jnp.abs(gates))))
            for u, (k, q, least, live) in enumerate(units):
                ku, vu = take(k == 0, k0, k1), take(k == 0, v0, v1)
                wk.append(jnp.concatenate([take(q == 0, ku, zero), take(q == 0, zero, ku)], axis=1).astype(BF16))
                wv.append(jnp.concatenate([take(q == 0, vu, zero), take(q == 0, zero, vu)], axis=1).astype(BF16))
                kt = ku.T
                columns = pl.ds(pl.multiple_of(where * 256 + u * SPAN, SPAN), SPAN)
                wt_all[0:128, columns] = take(q == 0, kt, zero).astype(BF16)
                wt_all[128:256, columns] = take(q == 0, zero, kt).astype(BF16)
                column = jnp.broadcast_to(take(k == 0, evict[0:1, :], evict[1:2, :]), (SPAN, SPAN)).T
                bias = jnp.where(lag >= least, column, 0.0)
                if s is not CROSS:
                    bias = jnp.where(lag >= live, bias, NEG)
                todo.append((s, u, bias))
        wk, wv = jnp.concatenate(wk, axis=0), jnp.concatenate(wv, axis=0)
        height = len(todo) * SPAN
        for c in range(4):
            cols = slice(c * 256, (c + 1) * 256)
            raw_s[c, 0:height, :] = jnp.dot(wk, qct[:, cols], preferred_element_type=F32)
            raw_g[c, 0:height, :] = jnp.dot(wv, oct_[:, cols], preferred_element_type=F32)
            for at, (s, u, bias) in enumerate(todo):
                rows = slice(at * SPAN, (at + 1) * SPAN)
                for h in range(2):
                    lane = slice(h * SPAN, (h + 1) * SPAN)
                    wide = slice(c * 256 + h * SPAN, c * 256 + (h + 1) * SPAN)
                    score = (raw_s[c, rows, lane] * (SCALE * LOG2E) + bias).reshape(16, 8, SPAN)
                    grad = raw_g[c, rows, lane]
                    top = jnp.max(score, axis=0)
                    e = jnp.exp2(score - top[None])
                    e_all[2 * s + u, :, wide] = e.reshape(SPAN, SPAN)
                    p_all[2 * s + u, :, wide] = grad
                    stat[2 * s + u, 0, :, wide] = top
                    stat[2 * s + u, 1, :, wide] = jnp.sum(e, axis=0)
                    stat[2 * s + u, 2, :, wide] = jnp.sum(e * grad.reshape(16, 8, SPAN), axis=0)

    def first_pass(work, i, _):
        one, two = table(FIRST[0], i), table(FIRST[1], i)

        @pl.when(i == 0)
        def _():
            arrive(1)

        @pl.when(i == 1)
        def _():
            arrive(2, 0)
            send(2, 4, 0, right)
            arrive(6, 1)
            send(6, 4, 1, left)
            for part in range(2):
                arrive(8, part)
                send(8, 10, part, right)
                send(8, 14, part, left)
            arrive(2, 1)
            pass_on(2)
            arrive(6, 0)
            pass_on(6)
            pass_on(8)

        @pl.when(i == 2)
        def _():
            arrive(3)

        @pl.when(i == 3)
        def _():
            for part in range(2):
                arrive(4, part)
                send(4, 12, part, across)
            pass_on(4)
            arrive(7)
            arrive(9)

        @pl.when(i == 4)
        def _():
            arrive(5)

        @pl.when(i == 5)
        def _():
            for slot in (10, 14):
                arrive(slot)
                pass_on(slot)

        @pl.when(i == 6)
        def _():
            arrive(12)
            pass_on(12)
            arrive(11)
            arrive(15)

        @pl.when(i == 7)
        def _():
            arrive(13)

        scores_of(work, [(one, one, pairs(one)), (two, two, pairs(two))])
        return 0

    def first(q_in, o_in, qct, oct_, raw_s, raw_g):
        loads = [
            pltpu.make_async_copy(k_ref, blocks.at[0, pl.ds(0, 256)], in_sem.at[0]),
            pltpu.make_async_copy(v_ref, blocks.at[0, pl.ds(256, 256)], in_sem.at[1]),
            pltpu.make_async_copy(q_ref, q_in, in_sem.at[2]),
            pltpu.make_async_copy(o_ref, o_in, in_sem.at[3]),
        ]
        for load in loads:
            load.start()
        gate_row = gate_ref[...].astype(F32)
        blocks[0, 512:528, :] = jnp.concatenate(
            [gate_row[:, 0:128], gate_row[:, 128:256], jnp.zeros((14, SPAN), F32)], axis=0).astype(BF16)
        pl.semaphore_wait(barrier, 4)

        loads[0].wait()
        send(0, 2, 0, right)
        send(0, 8, 0, across)
        loads[1].wait()
        send(0, 6, 1, left)
        send(0, 2, 1, right)
        send(0, 8, 1, across)
        send(0, 6, 0, left)
        for part in range(2):
            send(0, 1, part, partner)

        loads[2].wait()
        loads[3].wait()
        for h in range(HEADS):
            wide = slice(h * SPAN, (h + 1) * SPAN)
            for q in range(2):
                part = slice(q * SPAN, (q + 1) * SPAN)
                for src, plain, turned in ((q_in, qc, qct), (o_in, oc, oct_)):
                    tile = src[part, wide]
                    plain[wide, part] = tile
                    turned[part, wide] = tile.T

        work = (qct, oct_, raw_s, raw_g)
        scores_of(work, [(CROSS, 0, pair_across())])
        lax.fori_loop(0, 8, functools.partial(first_pass, work), 0)

    turned, raw = pltpu.VMEM((2 * SPAN, WIDE), BF16), pltpu.VMEM((4, 512, 256), F32)
    pl.run_scoped(first, turned, turned, turned, turned, raw, raw)

    queries_of = [q for s in range(CROSS) for _, q, _, _ in pairs(s)] + [q_high]

    def combine(c, _):
        cols = pl.ds(pl.multiple_of(c * 256, 256), 256)
        tops = [jnp.full((8, 256), NEG, F32)] * 2
        for n, q in enumerate(queries_of):
            mine = stat[n, 0, :, cols]
            tops = [take(q == half, jnp.maximum(top, mine), top) for half, top in enumerate(tops)]
        tops = [jnp.broadcast_to(jnp.max(top, axis=0, keepdims=True), (8, 256)) for top in tops]
        mass = [jnp.zeros((8, 256), F32)] * 2
        weighted = [jnp.zeros((8, 256), F32)] * 2
        for n, q in enumerate(queries_of):
            factor = jnp.exp2(stat[n, 0, :, cols] - take(q == 0, tops[0], tops[1]))
            stat[n, 0, :, cols] = factor
            more = factor * stat[n, 1, :, cols]
            mass = [take(q == half, was + more, was) for half, was in enumerate(mass)]
            more = factor * stat[n, 2, :, cols]
            weighted = [take(q == half, was + more, was) for half, was in enumerate(weighted)]
        for half in range(2):
            inverse = 1.0 / jnp.broadcast_to(jnp.sum(mass[half], axis=0, keepdims=True), (8, 256))
            total[half, :, cols] = inverse
            total[2 + half, :, cols] = inverse * jnp.broadcast_to(jnp.sum(weighted[half], axis=0, keepdims=True), (8, 256))
        return 0

    lax.fori_loop(0, 4, combine, 0)

    def rows_of(part):
        return slice(part * SPAN, (part + 1) * SPAN)

    def pack(dst, part, rows, gate_rows):
        dst[rows_of(part), :] = rows[rows_of(part), :].astype(BF16)
        if part == 3:
            high = gate_rows[...].astype(BF16).astype(F32)
            dst[512:528, :] = jnp.concatenate([high, gate_rows[...] - high], axis=0).astype(BF16)

    def add(rows, gate_rows, part, src):
        rows[rows_of(part), :] = rows[rows_of(part), :] + src[rows_of(part), :].astype(F32)
        if part == 3:
            tail = src[512:528, :].astype(F32)
            gate_rows[...] = gate_rows[...] + tail[0:8] + tail[8:16]

    def leave(j, part, rows, gate_rows):
        pack(sum_out.at[j - 1], part, rows, gate_rows)
        sum_copy(j, part).start()

    def join(j, parts, others):
        rows, gate_rows = held.at[j - 1], held_gate.at[j - 1]
        for part in parts:
            for other in others:
                sum_copy(other, part).wait_recv()
                add(rows, gate_rows, part, sum_in.at[other - 1])
            leave(j, part, rows, gate_rows)

    def gradients_of(prob_low, grad_low, ds_all, place_at, group):
        todo = []
        for s, units in group:
            for u, (k, q, least, _) in enumerate(units):
                todo.append((2 * s + u, q == 0))
        height = len(todo) * SPAN
        gate_acc = [jnp.zeros((SPAN, SPAN), F32) for _ in todo]
        for c in range(4):
            cols = slice(c * 256, (c + 1) * 256)
            for at, (n, first) in enumerate(todo):
                factor = stat[n, 0, :, cols] * take(first, total[0, :, cols], total[1, :, cols])
                delta = take(first, total[2, :, cols], total[3, :, cols])
                prob = e_all[n, :, cols] * jnp.concatenate([factor] * 16, axis=0)
                grad = prob * (p_all[n, :, cols] - jnp.concatenate([delta] * 16, axis=0))
                gate_acc[at] = gate_acc[at] + grad[:, 0:128] + grad[:, 128:256]
                prob_low[at * SPAN:(at + 1) * SPAN, cols] = prob.astype(BF16)
                low = grad.astype(BF16)
                grad_low[at * SPAN:(at + 1) * SPAN, cols] = low
                ds_all[pl.ds(pl.multiple_of(place_at + at * SPAN, SPAN), SPAN), cols] = low
        value_acc = jnp.dot(prob_low[0:height, :], oc[...], preferred_element_type=F32)
        key_acc = jnp.dot(grad_low[0:height, :], qc[...], preferred_element_type=F32)
        zero = jnp.zeros((SPAN, SPAN), F32)
        at = 0
        for n, (s, units) in enumerate(group):
            key_out, value_out = [zero, zero], [zero, zero]
            gate_out = [jnp.zeros((1, SPAN), F32), jnp.zeros((1, SPAN), F32)]
            for k, q, least, _ in units:
                part = slice(at * SPAN, (at + 1) * SPAN)
                key_u = take(q == 0, key_acc[part, 0:128], key_acc[part, 128:256]) * SCALE
                value_u = take(q == 0, value_acc[part, 0:128], value_acc[part, 128:256])
                gate_u = jnp.sum(jnp.where(lag >= least, gate_acc[at], 0.0).T, axis=0, keepdims=True)
                for half in range(2):
                    hit = k == half
                    key_out[half] = key_out[half] + take(hit, key_u, zero)
                    value_out[half] = value_out[half] + take(hit, value_u, zero)
                    gate_out[half] = gate_out[half] + take(hit, gate_u, jnp.zeros((1, SPAN), F32))
                at += 1
            cur[n, 0:128, :] = key_out[0]
            cur[n, 128:256, :] = key_out[1]
            cur[n, 256:384, :] = value_out[0]
            cur[n, 384:512, :] = value_out[1]
            cur_gate[n] = jnp.concatenate(gate_out + [jnp.zeros((6, SPAN), F32)], axis=0)

    def to_partner(j, n):
        for part in range(4):
            pack(pre_out.at[j], part, cur.at[n], cur_gate.at[n])
        pre_copy(j).start()

    def from_partner(j, n):
        pre_copy(j).wait_recv()
        for part in range(4):
            add(cur.at[n], cur_gate.at[n], part, pre_in.at[j])

    def second_pass(prob_low, grad_low, ds_all, i, _):
        one, two = table(SECOND[0], i), table(SECOND[1], i)
        gradients_of(prob_low, grad_low, ds_all, i * 512, [(one, pairs(one)), (two, pairs(two))])

        @pl.when(i <= 6)
        def _():
            to_partner(lax.div(two, 2), 1)

        @pl.when(i == 0)
        def _():
            to_partner(lax.div(one, 2), 0)

        @pl.when(i >= 1)
        def _():
            from_partner(lax.div(one, 2), 0)

        @pl.when(i == 6)
        def _():
            join(2, (2, 3), (6,))

        for at in range(1, CHIPS):
            @pl.when(one == 2 * at)
            def _():
                for part in range(4):
                    if at in (5, 6, 7) or (at, part // 2) in ((1, 1), (3, 0)):
                        leave(at, part, cur.at[0], cur_gate.at[0])
                if at in (1, 2, 3, 4):
                    held[at - 1] = cur[0]
                    held_gate[at - 1] = cur_gate[0]

        @pl.when(i == 5)
        def _():
            join(2, (0, 1), (6,))

        @pl.when(i == 7)
        def _():
            own[...] = cur[1]
            own_gate[...] = cur_gate[1]

        return 0

    def query_pass(ds_all, c, _):
        @pl.when(c == 1)
        def _():
            join(4, (2, 3), (5, 7))

        @pl.when(c == 2)
        def _():
            join(1, (0, 1), (2,))
            join(3, (2, 3), (2,))

        cols = pl.ds(pl.multiple_of(c * 256, 256), 256)
        acc = jnp.dot(wt_all[...], ds_all[:, cols], preferred_element_type=F32) * SCALE
        for q in range(2):
            for h in range(2):
                tile = acc[q * SPAN:(q + 1) * SPAN, h * SPAN:(h + 1) * SPAN].T
                lanes = pl.ds(pl.multiple_of(c * 256 + h * SPAN, SPAN), SPAN)
                dq_ref[q * SPAN:(q + 1) * SPAN, lanes] = tile.astype(BF16)
        return 0

    def second(prob_low, grad_low, ds_all):
        lax.fori_loop(0, 8, functools.partial(second_pass, prob_low, grad_low, ds_all), 0)
        gradients_of(prob_low, grad_low, ds_all, CROSS * 256, [(CROSS, pair_across())])
        own[...] = own[...] + cur[0]
        own_gate[...] = own_gate[...] + cur_gate[0]
        join(4, (0, 1), (5, 7))
        lax.fori_loop(0, 4, functools.partial(query_pass, ds_all), 0)

    pl.run_scoped(second, pltpu.VMEM((512, WIDE), BF16), pltpu.VMEM((512, WIDE), BF16), pltpu.VMEM((PAIRS * SPAN, WIDE), BF16))

    pre_copy(0).wait_recv()
    for part in range(4):
        add(own, own_gate, part, pre_in.at[0])
    for j in (4, 1, 3):
        for part in range(4):
            sum_copy(j, part).wait_recv()
            add(own, own_gate, part, sum_in.at[j - 1])
    dk_ref[...] = own[0:256, :].astype(BF16)
    dv_ref[...] = own[256:512, :].astype(BF16)
    gate_sum = jnp.concatenate([own_gate[0:1, :], own_gate[1:2, :]], axis=1)
    dg_ref[...] = -gate_sum / (1.0 + jnp.exp(-gate_ref[...].astype(F32)))

    for sent, sem in ((blocks.at[pl.ds(0, 15)], block_send), (pre_out, pre_send), (sum_out, sum_send)):
        pltpu.make_async_remote_copy(
            src_ref=sent, dst_ref=sent, send_sem=sem, recv_sem=block_recv.at[0],
            device_id={"ctx": partner}, device_id_type=MESH).wait_send()


def hand_over(*refs):
    copies = [pltpu.make_async_copy(refs[n], refs[4 + n], refs[8].at[n]) for n in range(4)]
    for copy in copies:
        copy.start()
    for copy in copies:
        copy.wait()


def on_device(queries, keys, values, gate_logit, out_grad, stretch_place):
    rows = 2 * SPAN
    vmem = pl.BlockSpec(memory_space=pltpu.VMEM)
    anywhere = pl.BlockSpec(memory_space=pl.ANY)
    dma = pltpu.SemaphoreType.DMA
    outs = (
        jax.ShapeDtypeStruct((rows, WIDE), BF16),
        jax.ShapeDtypeStruct((rows, SPAN), BF16),
        jax.ShapeDtypeStruct((rows, SPAN), BF16),
        jax.ShapeDtypeStruct((1, rows), F32),
    )
    results = pl.pallas_call(
        kernel,
        out_shape=tuple(pltpu.VMEM(out.shape, out.dtype) for out in outs),
        in_specs=[pl.BlockSpec(memory_space=pltpu.SMEM), anywhere, anywhere, anywhere, vmem, anywhere],
        out_specs=(vmem,) * 4,
        scratch_shapes=[
            pltpu.VMEM((2 * CHIPS, ROWS, SPAN), BF16),
            pltpu.VMEM((WIDE, rows), BF16),
            pltpu.VMEM((WIDE, rows), BF16),
            pltpu.VMEM((rows, PAIRS * SPAN), BF16),
            pltpu.VMEM((PAIRS, SPAN, WIDE), F32),
            pltpu.VMEM((PAIRS, SPAN, WIDE), F32),
            pltpu.VMEM((PAIRS, 3, 8, WIDE), F32),
            pltpu.VMEM((4, 8, WIDE), F32),
            pltpu.VMEM((2, 2 * rows, SPAN), F32),
            pltpu.VMEM((2, 8, SPAN), F32),
            pltpu.VMEM((2 * rows, SPAN), F32),
            pltpu.VMEM((8, SPAN), F32),
            pltpu.VMEM((4, 2 * rows, SPAN), F32),
            pltpu.VMEM((4, 8, SPAN), F32),
            pltpu.VMEM((CHIPS, ROWS, SPAN), BF16),
            pltpu.VMEM((CHIPS, ROWS, SPAN), BF16),
            pltpu.VMEM((CHIPS - 1, ROWS, SPAN), BF16),
            pltpu.VMEM((CHIPS - 1, ROWS, SPAN), BF16),
            dma((4,)), dma, dma((21,)), dma, dma((CHIPS,)), dma, dma((CHIPS - 1, 4)),
        ],
        compiler_params=pltpu.CompilerParams(
            collective_id=0, has_side_effects=True, vmem_limit_bytes=63 * 1024 * 1024),
    )(stretch_place, queries, keys, values, gate_logit.T, out_grad)
    dq, dk, dv, dg = pl.pallas_call(
        hand_over,
        out_shape=outs,
        in_specs=[vmem] * 4,
        out_specs=(anywhere,) * 4,
        scratch_shapes=[dma((4,))],
        compiler_params=pltpu.CompilerParams(vmem_limit_bytes=1024 * 1024),
    )(*results)
    return dq, dk, dv, dg.T


def solution(mesh):
    whole = P("ctx", "head")
    return jax.shard_map(
        on_device, mesh=mesh, in_specs=(whole,) * 5 + (P(),), out_specs=(whole,) * 4, check_vma=False)
```

```python
import functools

import jax
import jax.numpy as jnp
from jax import lax
from jax.experimental import pallas as pl
from jax.experimental.pallas import tpu as pltpu
from jax.sharding import PartitionSpec as P

DELAY = 256
SPAN = 128
HEADS = 8
WIDE = SPAN * HEADS
CHIPS = 8
ROWS = 528
NEG = -1e30
LOG2E = 1.4426950408889634
SCALE = 128 ** (-0.5)
MESH = pl.DeviceIdType.MESH
F32, BF16 = jnp.float32, jnp.bfloat16


FIRST = ((0, 2, 8, 7, 4, 10, 11), (1, 6, 3, 9, 5, 14, 15))
SECOND = ((13, 12, 5, 4, 8, 2, 6), (11, 10, 9, 3, 7, 1, 0))
CROSS = 16
LATER = tuple(29 - s if s in (14, 15) else 2 * (SECOND[0] if s in SECOND[0] else SECOND[1]).index(s) + (s in SECOND[1])
              for s in range(CROSS))
PAIRS = 33
PARTS = (pl.ds(0, 256), pl.ds(256, 272))
QUARTERS = (pl.ds(0, 128), pl.ds(128, 128), pl.ds(256, 128), pl.ds(384, 144))


def table(values, i):
    out = i * 0 + values[0]
    for at, value in enumerate(values[1:], 1):
        out = jnp.where(i == at, value, out)
    return out


def chip_at(y, x, j, sign):
    dy, dx = (j // 4, j % 4) if isinstance(j, int) else (lax.div(j, 4), lax.rem(j, 4))
    return lax.rem(y + 2 + sign * dy, 2) * 4 + lax.rem(x + 4 + sign * dx, 4)


def kernel(
    place, q_ref, k_ref, v_ref, gate_ref, o_ref,
    dq_ref, dk_ref, dv_ref, dg_ref,
    blocks, qc, oc, wt_all, e_all, p_all, stat, total,
    cur, cur_gate, own, own_gate, held, held_gate, pre_out, pre_in, sum_out, sum_in,
    in_sem, block_send, block_recv, pre_send, pre_recv, sum_send, sum_recv,
):
    me = lax.axis_index("ctx")
    core = lax.rem(me, 2)
    chip = lax.div(me, 2)
    y, x = lax.div(chip, 4), lax.rem(chip, 4)
    partner = me + 1 - 2 * core
    right = chip_at(y, x, 1, 1) * 2 + core
    left = chip_at(y, x, 1, -1) * 2 + core
    across = chip_at(y, x, 4, 1) * 2 + core

    barrier = pltpu.get_barrier_semaphore()
    for other in (partner, right, left, across):
        pl.semaphore_signal(barrier, inc=1, device_id={"ctx": other}, device_id_type=MESH)

    def recv_sem(slot, part):
        return block_recv.at[16 + slot // 2 if part == 1 and slot in (2, 4, 6, 8) else slot]

    def send(source, slot, part, target):
        pltpu.make_async_remote_copy(
            src_ref=blocks.at[source, PARTS[part]], dst_ref=blocks.at[slot, PARTS[part]], send_sem=block_send,
            recv_sem=recv_sem(slot, part), device_id={"ctx": target}, device_id_type=MESH).start()

    def arrive(slot, part=None):
        where = blocks.at[slot] if part is None else blocks.at[slot, PARTS[part]]
        pltpu.make_async_remote_copy(
            src_ref=where, dst_ref=where, send_sem=block_send, recv_sem=recv_sem(slot, part or 0),
            device_id={"ctx": partner}, device_id_type=MESH).wait_recv()

    def pass_on(slot):
        for part in range(2):
            send(slot, slot + 1, part, partner)

    def pre_copy(j):
        return pltpu.make_async_remote_copy(
            src_ref=pre_out.at[j], dst_ref=pre_in.at[j], send_sem=pre_send,
            recv_sem=pre_recv.at[j], device_id={"ctx": partner}, device_id_type=MESH)

    def sum_copy(j, part):
        target = {1: left, 2: left if part < 2 else right, 3: right, 4: across, 5: left, 6: across, 7: right}[j]
        return pltpu.make_async_remote_copy(
            src_ref=sum_out.at[j - 1, QUARTERS[part]], dst_ref=sum_in.at[j - 1, QUARTERS[part]], send_sem=sum_send,
            recv_sem=sum_recv.at[j - 1, part], device_id={"ctx": target}, device_id_type=MESH)

    key_row = lax.broadcasted_iota(jnp.int32, (SPAN, SPAN), 0)
    query_col = lax.broadcasted_iota(jnp.int32, (SPAN, SPAN), 1)
    lag = query_col - key_row
    a0, a1 = place[2 * me], place[2 * me + 1]
    a_low = jnp.minimum(a0, a1)
    q_high = (a1 > a0).astype(jnp.int32)

    def block_of(slot):
        theirs = chip_at(y, x, lax.div(slot, 2), -1) * 2 + lax.rem(core + slot, 2)
        b0, b1 = place[2 * theirs], place[2 * theirs + 1]
        return b0, b1, (b1 < b0).astype(jnp.int32)

    def described(k, q, b0, b1):
        apart = jnp.where(q == 0, a0, a1) - jnp.where(k == 0, b0, b1)
        return k, q, DELAY - SPAN * apart, -SPAN * apart

    def pairs(s):
        b0, b1, k_low = block_of(s)
        below = jnp.minimum(b0, b1) < a_low
        diag = s == 0
        k0 = jnp.where(diag, 0, jnp.where(below, k_low, 0))
        k1 = jnp.where(diag, 1, jnp.where(below, k_low, 1))
        q0 = jnp.where(diag, 0, jnp.where(below, 1 - q_high, q_high))
        q1 = jnp.where(diag, 1, q_high)
        return described(k0, q0, b0, b1), described(k1, q1, b0, b1)

    def pair_across():
        b0, b1, k_low = block_of(core * 0)
        return (described(k_low, q_high, b0, b1),)

    def take(first, a, b):
        return lax.select(first, a, b)

    def scores_of(work, group):
        qct, oct_, raw_s, raw_g = work
        zero = jnp.zeros((SPAN, SPAN), F32)
        wk, wv, todo = [], [], []
        for s, slot, units in group:
            where = s if s is CROSS else table(LATER, s)
            k0, k1 = blocks[slot, 0:128, :].astype(F32), blocks[slot, 128:256, :].astype(F32)
            v0, v1 = blocks[slot, 256:384, :].astype(F32), blocks[slot, 384:512, :].astype(F32)
            gates = blocks[slot, 512:528, :].astype(F32)
            evict = -LOG2E * (jnp.maximum(gates, 0.0) + jnp.log(1.0 + jnp.exp(-jnp.abs(gates))))
            for u, (k, q, least, live) in enumerate(units):
                ku, vu = take(k == 0, k0, k1), take(k == 0, v0, v1)
                wk.append(jnp.concatenate([take(q == 0, ku, zero), take(q == 0, zero, ku)], axis=1).astype(BF16))
                wv.append(jnp.concatenate([take(q == 0, vu, zero), take(q == 0, zero, vu)], axis=1).astype(BF16))
                kt = ku.T
                columns = pl.ds(pl.multiple_of(where * 256 + u * SPAN, SPAN), SPAN)
                wt_all[0:128, columns] = take(q == 0, kt, zero).astype(BF16)
                wt_all[128:256, columns] = take(q == 0, zero, kt).astype(BF16)
                column = jnp.broadcast_to(take(k == 0, evict[0:1, :], evict[1:2, :]), (SPAN, SPAN)).T
                bias = jnp.where(lag >= least, column, 0.0)
                if s is not CROSS:
                    bias = jnp.where(lag >= live, bias, NEG)
                todo.append((s, u, bias))
        wk, wv = jnp.concatenate(wk, axis=0), jnp.concatenate(wv, axis=0)
        height = len(todo) * SPAN
        for c in range(4):
            cols = slice(c * 256, (c + 1) * 256)
            raw_s[c, 0:height, :] = jnp.dot(wk, qct[:, cols], preferred_element_type=F32)
            raw_g[c, 0:height, :] = jnp.dot(wv, oct_[:, cols], preferred_element_type=F32)
            for at, (s, u, bias) in enumerate(todo):
                rows = slice(at * SPAN, (at + 1) * SPAN)
                for h in range(2):
                    lane = slice(h * SPAN, (h + 1) * SPAN)
                    wide = slice(c * 256 + h * SPAN, c * 256 + (h + 1) * SPAN)
                    score = (raw_s[c, rows, lane] * (SCALE * LOG2E) + bias).reshape(16, 8, SPAN)
                    grad = raw_g[c, rows, lane]
                    top = jnp.max(score, axis=0)
                    e = jnp.exp2(score - top[None])
                    e_all[2 * s + u, :, wide] = e.reshape(SPAN, SPAN)
                    p_all[2 * s + u, :, wide] = grad
                    stat[2 * s + u, 0, :, wide] = top
                    stat[2 * s + u, 1, :, wide] = jnp.sum(e, axis=0)
                    stat[2 * s + u, 2, :, wide] = jnp.sum(e * grad.reshape(16, 8, SPAN), axis=0)

    def first_pass(work, i, _):
        one, two = table(FIRST[0], i), table(FIRST[1], i)

        @pl.when(i == 0)
        def _():
            arrive(1)

        @pl.when(i == 1)
        def _():
            arrive(2, 0)
            send(2, 4, 0, right)
            arrive(6, 1)
            send(6, 4, 1, left)
            for part in range(2):
                arrive(8, part)
                send(8, 10, part, right)
                send(8, 14, part, left)
            arrive(2, 1)
            pass_on(2)
            arrive(6, 0)
            pass_on(6)
            pass_on(8)

        @pl.when(i == 2)
        def _():
            arrive(3)

        @pl.when(i == 3)
        def _():
            for part in range(2):
                arrive(4, part)
                send(4, 12, part, across)
            pass_on(4)
            arrive(7)
            arrive(9)

        @pl.when(i == 4)
        def _():
            arrive(5)

        @pl.when(i == 5)
        def _():
            for slot in (10, 14):
                arrive(slot)
                pass_on(slot)

        @pl.when(i == 6)
        def _():
            arrive(12)
            pass_on(12)
            arrive(11)
            arrive(15)

        scores_of(work, [(one, one, pairs(one)), (two, two, pairs(two))])
        return 0

    def into(q, was, more, op):
        if q is None:
            return [was[0], op(was[1], more)]
        high = q == q_high
        return [take(high, was[0], op(was[0], more)), take(high, op(was[1], more), was[1])]

    def merge(units, fresh, c, _):
        cols = pl.ds(pl.multiple_of(c * 256, 256), 256)
        if fresh:
            old = [jnp.full((8, 256), NEG, F32)] * 2
            mass = weighted = [jnp.zeros((8, 256), F32)] * 2
        else:
            old, mass, weighted = ([total[2 * n + half, :, cols] for half in range(2)] for n in range(3))
        tops = old
        for n, q in units:
            mine = stat[n, 0, :, cols]
            tops = into(q, tops, mine, jnp.maximum)
        if not fresh:
            tops = [jnp.broadcast_to(jnp.max(top, axis=0, keepdims=True), (8, 256)) for top in tops]
            keep = [jnp.exp2(was - top) for was, top in zip(old, tops)]
            mass = [was * factor for was, factor in zip(mass, keep)]
            weighted = [was * factor for was, factor in zip(weighted, keep)]
        for n, q in units:
            factor = jnp.exp2(stat[n, 0, :, cols] - (tops[1] if q is None else take(q == q_high, tops[1], tops[0])))
            mass = into(q, mass, factor * stat[n, 1, :, cols], jnp.add)
            weighted = into(q, weighted, factor * stat[n, 2, :, cols], jnp.add)
        for half in range(2):
            total[half, :, cols] = tops[half]
            if fresh:
                total[2 + half, :, cols] = mass[half]
                total[4 + half, :, cols] = weighted[half]
            else:
                inverse = 1.0 / jnp.broadcast_to(jnp.sum(mass[half], axis=0, keepdims=True), (8, 256))
                total[2 + half, :, cols] = inverse
                total[4 + half, :, cols] = inverse * jnp.broadcast_to(
                    jnp.sum(weighted[half], axis=0, keepdims=True), (8, 256))
        return 0

    def units_of(steps):
        return [(2 * s + u, q if s == 0 or u == 0 else None) for s in steps for u, (_, q, _, _) in enumerate(pairs(s))]

    def first_last(work, i, _):
        s = 12 + i

        @pl.when(i == 1)
        def _():
            seen = units_of([s for s in range(CROSS) if s != 13]) + [(2 * CROSS, None)]
            lax.fori_loop(0, 4, functools.partial(merge, seen, True), 0)
            arrive(13)

        scores_of(work, [(s, s, pairs(s))])
        return 0

    def first(q_in, o_in, qct, oct_, raw_s, raw_g):
        loads = [
            pltpu.make_async_copy(k_ref, blocks.at[0, pl.ds(0, 256)], in_sem.at[0]),
            pltpu.make_async_copy(v_ref, blocks.at[0, pl.ds(256, 256)], in_sem.at[1]),
            pltpu.make_async_copy(q_ref, q_in, in_sem.at[2]),
            pltpu.make_async_copy(o_ref, o_in, in_sem.at[3]),
        ]
        for load in loads:
            load.start()
        gate_row = gate_ref[...].astype(F32)
        blocks[0, 512:528, :] = jnp.concatenate(
            [gate_row[:, 0:128], gate_row[:, 128:256], jnp.zeros((14, SPAN), F32)], axis=0).astype(BF16)
        pl.semaphore_wait(barrier, 4)

        loads[0].wait()
        send(0, 2, 0, right)
        send(0, 8, 0, across)
        loads[1].wait()
        send(0, 6, 1, left)
        send(0, 2, 1, right)
        send(0, 8, 1, across)
        send(0, 6, 0, left)
        for part in range(2):
            send(0, 1, part, partner)

        loads[2].wait()
        loads[3].wait()
        for h in range(HEADS):
            wide = slice(h * SPAN, (h + 1) * SPAN)
            for q in range(2):
                part = slice(q * SPAN, (q + 1) * SPAN)
                for src, plain, turned in ((q_in, qc, qct), (o_in, oc, oct_)):
                    tile = src[part, wide]
                    plain[wide, part] = tile
                    turned[part, wide] = tile.T

        work = (qct, oct_, raw_s, raw_g)
        scores_of(work, [(CROSS, 0, pair_across())])
        lax.fori_loop(0, 7, functools.partial(first_pass, work), 0)
        lax.fori_loop(0, 2, functools.partial(first_last, work), 0)

    turned, raw = pltpu.VMEM((2 * SPAN, WIDE), BF16), pltpu.VMEM((4, 512, 256), F32)
    pl.run_scoped(first, turned, turned, turned, turned, raw, raw)

    lax.fori_loop(0, 4, functools.partial(merge, units_of([13]), False), 0)

    def rows_of(part):
        return slice(part * SPAN, (part + 1) * SPAN)

    def pack(dst, part, rows, gate_rows):
        dst[rows_of(part), :] = rows[rows_of(part), :].astype(BF16)
        if part == 3:
            high = gate_rows[...].astype(BF16).astype(F32)
            dst[512:528, :] = jnp.concatenate([high, gate_rows[...] - high], axis=0).astype(BF16)

    def add(rows, gate_rows, part, src):
        rows[rows_of(part), :] = rows[rows_of(part), :] + src[rows_of(part), :].astype(F32)
        if part == 3:
            tail = src[512:528, :].astype(F32)
            gate_rows[...] = gate_rows[...] + tail[0:8] + tail[8:16]

    def leave(j, part, rows, gate_rows):
        pack(sum_out.at[j - 1], part, rows, gate_rows)
        sum_copy(j, part).start()

    def join(j, parts, others):
        rows, gate_rows = held.at[j - 1], held_gate.at[j - 1]
        for part in parts:
            for other in others:
                sum_copy(other, part).wait_recv()
                add(rows, gate_rows, part, sum_in.at[other - 1])
            leave(j, part, rows, gate_rows)

    def gradients_of(prob_low, grad_low, ds_all, place_at, group):
        todo = []
        for s, units in group:
            for u, (k, q, least, _) in enumerate(units):
                todo.append((2 * s + u, q != q_high))
        height = len(todo) * SPAN
        gate_acc = [jnp.zeros((SPAN, SPAN), F32) for _ in todo]
        for c in range(4):
            cols = slice(c * 256, (c + 1) * 256)
            for at, (n, first) in enumerate(todo):
                factor = jnp.exp2(stat[n, 0, :, cols] - take(first, total[0, :, cols], total[1, :, cols]))
                factor = factor * take(first, total[2, :, cols], total[3, :, cols])
                delta = take(first, total[4, :, cols], total[5, :, cols])
                prob = e_all[n, :, cols] * jnp.concatenate([factor] * 16, axis=0)
                grad = prob * (p_all[n, :, cols] - jnp.concatenate([delta] * 16, axis=0))
                gate_acc[at] = gate_acc[at] + grad[:, 0:128] + grad[:, 128:256]
                prob_low[at * SPAN:(at + 1) * SPAN, cols] = prob.astype(BF16)
                low = grad.astype(BF16)
                grad_low[at * SPAN:(at + 1) * SPAN, cols] = low
                ds_all[pl.ds(pl.multiple_of(place_at + at * SPAN, SPAN), SPAN), cols] = low
        value_acc = jnp.dot(prob_low[0:height, :], oc[...], preferred_element_type=F32)
        key_acc = jnp.dot(grad_low[0:height, :], qc[...], preferred_element_type=F32)
        zero = jnp.zeros((SPAN, SPAN), F32)
        at = 0
        for n, (s, units) in enumerate(group):
            key_out, value_out = [zero, zero], [zero, zero]
            gate_out = [jnp.zeros((1, SPAN), F32), jnp.zeros((1, SPAN), F32)]
            for k, q, least, _ in units:
                part = slice(at * SPAN, (at + 1) * SPAN)
                key_u = take(q == 0, key_acc[part, 0:128], key_acc[part, 128:256]) * SCALE
                value_u = take(q == 0, value_acc[part, 0:128], value_acc[part, 128:256])
                gate_u = jnp.sum(jnp.where(lag >= least, gate_acc[at], 0.0).T, axis=0, keepdims=True)
                for half in range(2):
                    hit = k == half
                    key_out[half] = key_out[half] + take(hit, key_u, zero)
                    value_out[half] = value_out[half] + take(hit, value_u, zero)
                    gate_out[half] = gate_out[half] + take(hit, gate_u, jnp.zeros((1, SPAN), F32))
                at += 1
            cur[n, 0:128, :] = key_out[0]
            cur[n, 128:256, :] = key_out[1]
            cur[n, 256:384, :] = value_out[0]
            cur[n, 384:512, :] = value_out[1]
            cur_gate[n] = jnp.concatenate(gate_out + [jnp.zeros((6, SPAN), F32)], axis=0)

    def to_partner(j, n):
        for part in range(4):
            pack(pre_out.at[j], part, cur.at[n], cur_gate.at[n])
        pre_copy(j).start()

    def from_partner(j, n):
        pre_copy(j).wait_recv()
        for part in range(4):
            add(cur.at[n], cur_gate.at[n], part, pre_in.at[j])

    def second_pass(prob_low, grad_low, ds_all, i, _):
        one, two = table(SECOND[0], i), table(SECOND[1], i)
        gradients_of(prob_low, grad_low, ds_all, i * 512, [(one, pairs(one)), (two, pairs(two))])

        @pl.when(i == 0)
        def _():
            to_partner(6, 0)
            to_partner(5, 1)

        @pl.when(i == 1)
        def _():
            for j, n in ((6, 0), (5, 1)):
                from_partner(j, n)
                for part in range(4):
                    leave(j, part, cur.at[n], cur_gate.at[n])

        @pl.when(i <= 1)
        def _():
            s = 15 - i
            gradients_of(prob_low, grad_low, ds_all, 14 * 256 + i * 256, [(s, pairs(s))])

            @pl.when(i == 0)
            def _():
                to_partner(7, 0)

            @pl.when(i == 1)
            def _():
                from_partner(7, 0)
                for part in range(4):
                    leave(7, part, cur.at[0], cur_gate.at[0])

        @pl.when(i == 2)
        def _():
            to_partner(2, 0)
            to_partner(4, 1)

        for at, j, mine in ((3, 1, 2), (4, 3, 4), (5, 0, 1), (6, None, 3)):
            @pl.when(i == at)
            def _():
                if j is not None:
                    to_partner(j, 1)
                if at == 5:
                    join(2, (2, 3), (6,))
                from_partner(mine, 0)
                for part in range(4):
                    if (mine, part // 2) in ((1, 1), (3, 0)):
                        leave(mine, part, cur.at[0], cur_gate.at[0])
                held[mine - 1] = cur[0]
                held_gate[mine - 1] = cur_gate[0]
                if at == 4:
                    join(2, (0, 1), (6,))
                if at == 6:
                    own[...] = cur[1]
                    own_gate[...] = cur_gate[1]

        return 0

    def query_pass(ds_all, c, _):
        @pl.when(c == 1)
        def _():
            join(1, (0, 1), (2,))
            join(3, (2, 3), (2,))

        cols = pl.ds(pl.multiple_of(c * 256, 256), 256)
        acc = jnp.dot(wt_all[...], ds_all[:, cols], preferred_element_type=F32) * SCALE
        for q in range(2):
            for h in range(2):
                tile = acc[q * SPAN:(q + 1) * SPAN, h * SPAN:(h + 1) * SPAN].T
                lanes = pl.ds(pl.multiple_of(c * 256 + h * SPAN, SPAN), SPAN)
                dq_ref[q * SPAN:(q + 1) * SPAN, lanes] = tile.astype(BF16)
        return 0

    def second(prob_low, grad_low, ds_all):
        lax.fori_loop(0, 7, functools.partial(second_pass, prob_low, grad_low, ds_all), 0)
        gradients_of(prob_low, grad_low, ds_all, CROSS * 256, [(CROSS, pair_across())])
        own[...] = own[...] + cur[0]
        own_gate[...] = own_gate[...] + cur_gate[0]
        join(4, (0, 1, 2, 3), (5, 7))
        lax.fori_loop(0, 4, functools.partial(query_pass, ds_all), 0)

    pl.run_scoped(second, pltpu.VMEM((512, WIDE), BF16), pltpu.VMEM((512, WIDE), BF16), pltpu.VMEM((PAIRS * SPAN, WIDE), BF16))

    pre_copy(0).wait_recv()
    for part in range(4):
        add(own, own_gate, part, pre_in.at[0])
    for j in (4, 1, 3):
        for part in range(4):
            sum_copy(j, part).wait_recv()
            add(own, own_gate, part, sum_in.at[j - 1])
    dk_ref[...] = own[0:256, :].astype(BF16)
    dv_ref[...] = own[256:512, :].astype(BF16)
    gate_sum = jnp.concatenate([own_gate[0:1, :], own_gate[1:2, :]], axis=1)
    dg_ref[...] = -gate_sum / (1.0 + jnp.exp(-gate_ref[...].astype(F32)))

    for sent, sem in ((blocks.at[pl.ds(0, 15)], block_send), (pre_out, pre_send), (sum_out, sum_send)):
        pltpu.make_async_remote_copy(
            src_ref=sent, dst_ref=sent, send_sem=sem, recv_sem=block_recv.at[0],
            device_id={"ctx": partner}, device_id_type=MESH).wait_send()


def hand_over(*refs):
    copies = [pltpu.make_async_copy(refs[n], refs[4 + n], refs[8].at[n]) for n in range(4)]
    for copy in copies:
        copy.start()
    for copy in copies:
        copy.wait()


def on_device(queries, keys, values, gate_logit, out_grad, stretch_place):
    rows = 2 * SPAN
    vmem = pl.BlockSpec(memory_space=pltpu.VMEM)
    anywhere = pl.BlockSpec(memory_space=pl.ANY)
    dma = pltpu.SemaphoreType.DMA
    outs = (
        jax.ShapeDtypeStruct((rows, WIDE), BF16),
        jax.ShapeDtypeStruct((rows, SPAN), BF16),
        jax.ShapeDtypeStruct((rows, SPAN), BF16),
        jax.ShapeDtypeStruct((1, rows), F32),
    )
    results = pl.pallas_call(
        kernel,
        out_shape=tuple(pltpu.VMEM(out.shape, out.dtype) for out in outs),
        in_specs=[pl.BlockSpec(memory_space=pltpu.SMEM), anywhere, anywhere, anywhere, vmem, anywhere],
        out_specs=(vmem,) * 4,
        scratch_shapes=[
            pltpu.VMEM((2 * CHIPS, ROWS, SPAN), BF16),
            pltpu.VMEM((WIDE, rows), BF16),
            pltpu.VMEM((WIDE, rows), BF16),
            pltpu.VMEM((rows, PAIRS * SPAN), BF16),
            pltpu.VMEM((PAIRS, SPAN, WIDE), F32),
            pltpu.VMEM((PAIRS, SPAN, WIDE), F32),
            pltpu.VMEM((PAIRS, 3, 8, WIDE), F32),
            pltpu.VMEM((6, 8, WIDE), F32),
            pltpu.VMEM((2, 2 * rows, SPAN), F32),
            pltpu.VMEM((2, 8, SPAN), F32),
            pltpu.VMEM((2 * rows, SPAN), F32),
            pltpu.VMEM((8, SPAN), F32),
            pltpu.VMEM((4, 2 * rows, SPAN), F32),
            pltpu.VMEM((4, 8, SPAN), F32),
            pltpu.VMEM((CHIPS, ROWS, SPAN), BF16),
            pltpu.VMEM((CHIPS, ROWS, SPAN), BF16),
            pltpu.VMEM((CHIPS - 1, ROWS, SPAN), BF16),
            pltpu.VMEM((CHIPS - 1, ROWS, SPAN), BF16),
            dma((4,)), dma, dma((21,)), dma, dma((CHIPS,)), dma, dma((CHIPS - 1, 4)),
        ],
        compiler_params=pltpu.CompilerParams(
            collective_id=0, has_side_effects=True, vmem_limit_bytes=63 * 1024 * 1024),
    )(stretch_place, queries, keys, values, gate_logit.T, out_grad)
    dq, dk, dv, dg = pl.pallas_call(
        hand_over,
        out_shape=outs,
        in_specs=[vmem] * 4,
        out_specs=(anywhere,) * 4,
        scratch_shapes=[dma((4,))],
        compiler_params=pltpu.CompilerParams(vmem_limit_bytes=1024 * 1024),
    )(*results)
    return dq, dk, dv, dg.T


def solution(mesh):
    whole = P("ctx", "head")
    return jax.shard_map(
        on_device, mesh=mesh, in_specs=(whole,) * 5 + (P(),), out_specs=(whole,) * 4, check_vma=False)
```

```python
import functools

import jax
import jax.numpy as jnp
from jax import lax
from jax.experimental import pallas as pl
from jax.experimental.pallas import tpu as pltpu
from jax.sharding import PartitionSpec as P

DELAY = 256
SPAN = 128
HEADS = 8
WIDE = SPAN * HEADS
CHIPS = 8
ROWS = 528
NEG = -1e30
LOG2E = 1.4426950408889634
SCALE = 128 ** (-0.5)
MESH = pl.DeviceIdType.MESH
F32, BF16 = jnp.float32, jnp.bfloat16


FIRST = ((0, 2, 8, 7, 4, 10, 11), (1, 6, 3, 9, 5, 14, 15))
SECOND = ((13, 12, 5, 4, 8, 2, 6), (11, 10, 9, 3, 7, 1, 0))
CROSS = 16
LATER = tuple(29 - s if s in (14, 15) else 2 * (SECOND[0] if s in SECOND[0] else SECOND[1]).index(s) + (s in SECOND[1])
              for s in range(CROSS))
PAIRS = 33
PARTS = (pl.ds(0, 256), pl.ds(256, 272))
QUARTERS = (pl.ds(0, 128), pl.ds(128, 128), pl.ds(256, 128), pl.ds(384, 144))


def table(values, i):
    out = i * 0 + values[0]
    for at, value in enumerate(values[1:], 1):
        out = jnp.where(i == at, value, out)
    return out


def chip_at(y, x, j, sign):
    dy, dx = (j // 4, j % 4) if isinstance(j, int) else (lax.div(j, 4), lax.rem(j, 4))
    return lax.rem(y + 2 + sign * dy, 2) * 4 + lax.rem(x + 4 + sign * dx, 4)


def kernel(
    place, q_ref, k_ref, v_ref, gate_ref, o_ref,
    dq_ref, dk_ref, dv_ref, dg_ref,
    blocks, qc, oc, wt_all, e_all, p_all, stat, total,
    cur, cur_gate, own, own_gate, held, held_gate, pre_out, pre_in, sum_out, sum_in,
    in_sem, block_send, block_recv, pre_send, pre_recv, sum_send, sum_recv,
):
    me = lax.axis_index("ctx")
    core = lax.rem(me, 2)
    chip = lax.div(me, 2)
    y, x = lax.div(chip, 4), lax.rem(chip, 4)
    partner = me + 1 - 2 * core
    right = chip_at(y, x, 1, 1) * 2 + core
    left = chip_at(y, x, 1, -1) * 2 + core
    across = chip_at(y, x, 4, 1) * 2 + core

    barrier = pltpu.get_barrier_semaphore()
    for other in (partner, right, left, across):
        pl.semaphore_signal(barrier, inc=1, device_id={"ctx": other}, device_id_type=MESH)

    def recv_sem(slot, part):
        return block_recv.at[16 + slot // 2 if part == 1 and slot in (2, 4, 6, 8) else slot]

    def send(source, slot, part, target):
        pltpu.make_async_remote_copy(
            src_ref=blocks.at[source, PARTS[part]], dst_ref=blocks.at[slot, PARTS[part]], send_sem=block_send,
            recv_sem=recv_sem(slot, part), device_id={"ctx": target}, device_id_type=MESH).start()

    def arrive(slot, part=None):
        where = blocks.at[slot] if part is None else blocks.at[slot, PARTS[part]]
        pltpu.make_async_remote_copy(
            src_ref=where, dst_ref=where, send_sem=block_send, recv_sem=recv_sem(slot, part or 0),
            device_id={"ctx": partner}, device_id_type=MESH).wait_recv()

    def quarter_copy(source, slot, quarter, target):
        sem = {(2, 0): 2, (2, 1): 21, (6, 2): 19, (6, 3): 22, (4, 0): 4, (4, 1): 23, (4, 2): 18, (4, 3): 24}
        return pltpu.make_async_remote_copy(
            src_ref=blocks.at[source, QUARTERS[quarter]], dst_ref=blocks.at[slot, QUARTERS[quarter]], send_sem=block_send,
            recv_sem=block_recv.at[sem.get((slot, quarter), slot)], device_id={"ctx": target}, device_id_type=MESH)

    def pass_on(slot):
        for part in range(2):
            send(slot, slot + 1, part, partner)

    def pre_copy(j):
        return pltpu.make_async_remote_copy(
            src_ref=pre_out.at[j], dst_ref=pre_in.at[j], send_sem=pre_send,
            recv_sem=pre_recv.at[j], device_id={"ctx": partner}, device_id_type=MESH)

    def sum_copy(j, part):
        target = {1: left, 2: left if part < 2 else right, 3: right, 4: across, 5: left, 6: across, 7: right}[j]
        return pltpu.make_async_remote_copy(
            src_ref=sum_out.at[j - 1, QUARTERS[part]], dst_ref=sum_in.at[j - 1, QUARTERS[part]], send_sem=sum_send,
            recv_sem=sum_recv.at[j - 1, part], device_id={"ctx": target}, device_id_type=MESH)

    key_row = lax.broadcasted_iota(jnp.int32, (SPAN, SPAN), 0)
    query_col = lax.broadcasted_iota(jnp.int32, (SPAN, SPAN), 1)
    lag = query_col - key_row
    a0, a1 = place[2 * me], place[2 * me + 1]
    a_low = jnp.minimum(a0, a1)
    q_high = (a1 > a0).astype(jnp.int32)

    def block_of(slot):
        theirs = chip_at(y, x, lax.div(slot, 2), -1) * 2 + lax.rem(core + slot, 2)
        b0, b1 = place[2 * theirs], place[2 * theirs + 1]
        return b0, b1, (b1 < b0).astype(jnp.int32)

    def described(k, q, b0, b1):
        apart = jnp.where(q == 0, a0, a1) - jnp.where(k == 0, b0, b1)
        return k, q, DELAY - SPAN * apart, -SPAN * apart

    def pairs(s):
        b0, b1, k_low = block_of(s)
        below = jnp.minimum(b0, b1) < a_low
        diag = s == 0
        k0 = jnp.where(diag, 0, jnp.where(below, k_low, 0))
        k1 = jnp.where(diag, 1, jnp.where(below, k_low, 1))
        q0 = jnp.where(diag, 0, jnp.where(below, 1 - q_high, q_high))
        q1 = jnp.where(diag, 1, q_high)
        return described(k0, q0, b0, b1), described(k1, q1, b0, b1)

    def pair_across():
        b0, b1, k_low = block_of(core * 0)
        return (described(k_low, q_high, b0, b1),)

    def take(first, a, b):
        return lax.select(first, a, b)

    def scores_of(work, group):
        qct, oct_, raw_s, raw_g = work
        zero = jnp.zeros((SPAN, SPAN), F32)
        wk, wv, todo = [], [], []
        for s, slot, units in group:
            where = s if s is CROSS else table(LATER, s)
            k0, k1 = blocks[slot, 0:128, :].astype(F32), blocks[slot, 128:256, :].astype(F32)
            v0, v1 = blocks[slot, 256:384, :].astype(F32), blocks[slot, 384:512, :].astype(F32)
            gates = blocks[slot, 512:528, :].astype(F32)
            evict = -LOG2E * (jnp.maximum(gates, 0.0) + jnp.log(1.0 + jnp.exp(-jnp.abs(gates))))
            for u, (k, q, least, live) in enumerate(units):
                ku, vu = take(k == 0, k0, k1), take(k == 0, v0, v1)
                wk.append(jnp.concatenate([take(q == 0, ku, zero), take(q == 0, zero, ku)], axis=1).astype(BF16))
                wv.append(jnp.concatenate([take(q == 0, vu, zero), take(q == 0, zero, vu)], axis=1).astype(BF16))
                kt = ku.T
                columns = pl.ds(pl.multiple_of(where * 256 + u * SPAN, SPAN), SPAN)
                wt_all[0:128, columns] = take(q == 0, kt, zero).astype(BF16)
                wt_all[128:256, columns] = take(q == 0, zero, kt).astype(BF16)
                column = jnp.broadcast_to(take(k == 0, evict[0:1, :], evict[1:2, :]), (SPAN, SPAN)).T
                bias = jnp.where(lag >= least, column, 0.0)
                if s is not CROSS:
                    bias = jnp.where(lag >= live, bias, NEG)
                todo.append((s, u, bias))
        wk, wv = jnp.concatenate(wk, axis=0), jnp.concatenate(wv, axis=0)
        height = len(todo) * SPAN
        for c in range(4):
            cols = slice(c * 256, (c + 1) * 256)
            raw_s[c, 0:height, :] = jnp.dot(wk, qct[:, cols], preferred_element_type=F32)
            raw_g[c, 0:height, :] = jnp.dot(wv, oct_[:, cols], preferred_element_type=F32)
            for at, (s, u, bias) in enumerate(todo):
                rows = slice(at * SPAN, (at + 1) * SPAN)
                for h in range(2):
                    lane = slice(h * SPAN, (h + 1) * SPAN)
                    wide = slice(c * 256 + h * SPAN, c * 256 + (h + 1) * SPAN)
                    score = (raw_s[c, rows, lane] * (SCALE * LOG2E) + bias).reshape(16, 8, SPAN)
                    grad = raw_g[c, rows, lane]
                    top = jnp.max(score, axis=0)
                    e = jnp.exp2(score - top[None])
                    e_all[2 * s + u, :, wide] = e.reshape(SPAN, SPAN)
                    p_all[2 * s + u, :, wide] = grad
                    stat[2 * s + u, 0, :, wide] = top
                    stat[2 * s + u, 1, :, wide] = jnp.sum(e, axis=0)
                    stat[2 * s + u, 2, :, wide] = jnp.sum(e * grad.reshape(16, 8, SPAN), axis=0)

    def first_pass(work, i, _):
        one, two = table(FIRST[0], i), table(FIRST[1], i)

        @pl.when(i == 0)
        def _():
            arrive(1)

        @pl.when(i == 1)
        def _():
            for quarter in (0, 1):
                quarter_copy(2, 2, quarter, partner).wait_recv()
                quarter_copy(2, 4, quarter, right).start()
                quarter_copy(6, 6, quarter + 2, partner).wait_recv()
                quarter_copy(6, 4, quarter + 2, left).start()
            for part in range(2):
                arrive(8, part)
                send(8, 10, part, right)
                send(8, 14, part, left)
            arrive(2, 1)
            pass_on(2)
            arrive(6, 0)
            pass_on(6)
            pass_on(8)

        @pl.when(i == 2)
        def _():
            arrive(3)
            for quarter in (0, 2):
                quarter_copy(4, 4, quarter, partner).wait_recv()
                quarter_copy(4, 12, quarter, across).start()

        @pl.when(i == 3)
        def _():
            for quarter in (1, 3):
                quarter_copy(4, 4, quarter, partner).wait_recv()
                quarter_copy(4, 12, quarter, across).start()
            pass_on(4)
            arrive(7)
            arrive(9)

        @pl.when(i == 4)
        def _():
            arrive(5)

        @pl.when(i == 5)
        def _():
            for slot in (10, 14):
                arrive(slot)
                pass_on(slot)

        @pl.when(i == 6)
        def _():
            arrive(12)
            pass_on(12)
            arrive(11)
            arrive(15)

        scores_of(work, [(one, one, pairs(one)), (two, two, pairs(two))])
        return 0

    def into(q, was, more, op):
        if q is None:
            return [was[0], op(was[1], more)]
        high = q == q_high
        return [take(high, was[0], op(was[0], more)), take(high, op(was[1], more), was[1])]

    def merge(units, fresh, c, _):
        cols = pl.ds(pl.multiple_of(c * 256, 256), 256)
        if fresh:
            old = [jnp.full((8, 256), NEG, F32)] * 2
            mass = weighted = [jnp.zeros((8, 256), F32)] * 2
        else:
            old, mass, weighted = ([total[2 * n + half, :, cols] for half in range(2)] for n in range(3))
        tops = old
        for n, q in units:
            mine = stat[n, 0, :, cols]
            tops = into(q, tops, mine, jnp.maximum)
        if not fresh:
            tops = [jnp.broadcast_to(jnp.max(top, axis=0, keepdims=True), (8, 256)) for top in tops]
            keep = [jnp.exp2(was - top) for was, top in zip(old, tops)]
            mass = [was * factor for was, factor in zip(mass, keep)]
            weighted = [was * factor for was, factor in zip(weighted, keep)]
        for n, q in units:
            factor = jnp.exp2(stat[n, 0, :, cols] - (tops[1] if q is None else take(q == q_high, tops[1], tops[0])))
            mass = into(q, mass, factor * stat[n, 1, :, cols], jnp.add)
            weighted = into(q, weighted, factor * stat[n, 2, :, cols], jnp.add)
        for half in range(2):
            total[half, :, cols] = tops[half]
            if fresh:
                total[2 + half, :, cols] = mass[half]
                total[4 + half, :, cols] = weighted[half]
            else:
                inverse = 1.0 / jnp.broadcast_to(jnp.sum(mass[half], axis=0, keepdims=True), (8, 256))
                total[2 + half, :, cols] = inverse
                total[4 + half, :, cols] = inverse * jnp.broadcast_to(
                    jnp.sum(weighted[half], axis=0, keepdims=True), (8, 256))
        return 0

    def units_of(steps):
        return [(2 * s + u, q if s == 0 or u == 0 else None) for s in steps for u, (_, q, _, _) in enumerate(pairs(s))]

    def first_last(work, i, _):
        s = 12 + i

        @pl.when(i == 1)
        def _():
            seen = units_of([s for s in range(CROSS) if s != 13]) + [(2 * CROSS, None)]
            lax.fori_loop(0, 4, functools.partial(merge, seen, True), 0)
            arrive(13)

        scores_of(work, [(s, s, pairs(s))])
        return 0

    def first(q_in, o_in, qct, oct_, raw_s, raw_g):
        loads = [
            pltpu.make_async_copy(k_ref, blocks.at[0, pl.ds(0, 256)], in_sem.at[0]),
            pltpu.make_async_copy(v_ref, blocks.at[0, pl.ds(256, 256)], in_sem.at[1]),
            pltpu.make_async_copy(q_ref, q_in, in_sem.at[2]),
            pltpu.make_async_copy(o_ref, o_in, in_sem.at[3]),
        ]
        for load in loads:
            load.start()
        gate_row = gate_ref[...].astype(F32)
        blocks[0, 512:528, :] = jnp.concatenate(
            [gate_row[:, 0:128], gate_row[:, 128:256], jnp.zeros((14, SPAN), F32)], axis=0).astype(BF16)
        pl.semaphore_wait(barrier, 4)

        loads[0].wait()
        for quarter in (0, 1):
            quarter_copy(0, 2, quarter, right).start()
        send(0, 8, 0, across)
        loads[1].wait()
        for quarter in (2, 3):
            quarter_copy(0, 6, quarter, left).start()
        send(0, 2, 1, right)
        send(0, 8, 1, across)
        send(0, 6, 0, left)
        for part in range(2):
            send(0, 1, part, partner)

        loads[2].wait()
        loads[3].wait()
        for h in range(HEADS):
            wide = slice(h * SPAN, (h + 1) * SPAN)
            for q in range(2):
                part = slice(q * SPAN, (q + 1) * SPAN)
                for src, plain, turned in ((q_in, qc, qct), (o_in, oc, oct_)):
                    tile = src[part, wide]
                    plain[wide, part] = tile
                    turned[part, wide] = tile.T

        work = (qct, oct_, raw_s, raw_g)
        scores_of(work, [(CROSS, 0, pair_across())])
        lax.fori_loop(0, 7, functools.partial(first_pass, work), 0)
        lax.fori_loop(0, 2, functools.partial(first_last, work), 0)

    turned, raw = pltpu.VMEM((2 * SPAN, WIDE), BF16), pltpu.VMEM((4, 512, 256), F32)
    pl.run_scoped(first, turned, turned, turned, turned, raw, raw)

    lax.fori_loop(0, 4, functools.partial(merge, units_of([13]), False), 0)

    def rows_of(part):
        return slice(part * SPAN, (part + 1) * SPAN)

    def pack(dst, part, rows, gate_rows):
        dst[rows_of(part), :] = rows[rows_of(part), :].astype(BF16)
        if part == 3:
            high = gate_rows[...].astype(BF16).astype(F32)
            dst[512:528, :] = jnp.concatenate([high, gate_rows[...] - high], axis=0).astype(BF16)

    def add(rows, gate_rows, part, src):
        rows[rows_of(part), :] = rows[rows_of(part), :] + src[rows_of(part), :].astype(F32)
        if part == 3:
            tail = src[512:528, :].astype(F32)
            gate_rows[...] = gate_rows[...] + tail[0:8] + tail[8:16]

    def leave(j, part, rows, gate_rows):
        pack(sum_out.at[j - 1], part, rows, gate_rows)
        sum_copy(j, part).start()

    def join(j, parts, others):
        rows, gate_rows = held.at[j - 1], held_gate.at[j - 1]
        for part in parts:
            for other in others:
                sum_copy(other, part).wait_recv()
                add(rows, gate_rows, part, sum_in.at[other - 1])
            leave(j, part, rows, gate_rows)

    def gradients_of(prob_low, grad_low, ds_all, place_at, group):
        todo = []
        for s, units in group:
            for u, (k, q, least, _) in enumerate(units):
                todo.append((2 * s + u, q != q_high))
        height = len(todo) * SPAN
        gate_acc = [jnp.zeros((SPAN, SPAN), F32) for _ in todo]
        for c in range(4):
            cols = slice(c * 256, (c + 1) * 256)
            for at, (n, first) in enumerate(todo):
                factor = jnp.exp2(stat[n, 0, :, cols] - take(first, total[0, :, cols], total[1, :, cols]))
                factor = factor * take(first, total[2, :, cols], total[3, :, cols])
                delta = take(first, total[4, :, cols], total[5, :, cols])
                prob = e_all[n, :, cols] * jnp.concatenate([factor] * 16, axis=0)
                grad = prob * (p_all[n, :, cols] - jnp.concatenate([delta] * 16, axis=0))
                gate_acc[at] = gate_acc[at] + grad[:, 0:128] + grad[:, 128:256]
                prob_low[at * SPAN:(at + 1) * SPAN, cols] = prob.astype(BF16)
                low = grad.astype(BF16)
                grad_low[at * SPAN:(at + 1) * SPAN, cols] = low
                ds_all[pl.ds(pl.multiple_of(place_at + at * SPAN, SPAN), SPAN), cols] = low
        value_acc = jnp.dot(prob_low[0:height, :], oc[...], preferred_element_type=F32)
        key_acc = jnp.dot(grad_low[0:height, :], qc[...], preferred_element_type=F32)
        zero = jnp.zeros((SPAN, SPAN), F32)
        at = 0
        for n, (s, units) in enumerate(group):
            key_out, value_out = [zero, zero], [zero, zero]
            gate_out = [jnp.zeros((1, SPAN), F32), jnp.zeros((1, SPAN), F32)]
            for k, q, least, _ in units:
                part = slice(at * SPAN, (at + 1) * SPAN)
                key_u = take(q == 0, key_acc[part, 0:128], key_acc[part, 128:256]) * SCALE
                value_u = take(q == 0, value_acc[part, 0:128], value_acc[part, 128:256])
                gate_u = jnp.sum(jnp.where(lag >= least, gate_acc[at], 0.0).T, axis=0, keepdims=True)
                for half in range(2):
                    hit = k == half
                    key_out[half] = key_out[half] + take(hit, key_u, zero)
                    value_out[half] = value_out[half] + take(hit, value_u, zero)
                    gate_out[half] = gate_out[half] + take(hit, gate_u, jnp.zeros((1, SPAN), F32))
                at += 1
            cur[n, 0:128, :] = key_out[0]
            cur[n, 128:256, :] = key_out[1]
            cur[n, 256:384, :] = value_out[0]
            cur[n, 384:512, :] = value_out[1]
            cur_gate[n] = jnp.concatenate(gate_out + [jnp.zeros((6, SPAN), F32)], axis=0)

    def to_partner(j, n):
        for part in range(4):
            pack(pre_out.at[j], part, cur.at[n], cur_gate.at[n])
        pre_copy(j).start()

    def from_partner(j, n):
        pre_copy(j).wait_recv()
        for part in range(4):
            add(cur.at[n], cur_gate.at[n], part, pre_in.at[j])

    def second_pass(prob_low, grad_low, ds_all, i, _):
        one, two = table(SECOND[0], i), table(SECOND[1], i)
        gradients_of(prob_low, grad_low, ds_all, i * 512, [(one, pairs(one)), (two, pairs(two))])

        @pl.when(i == 0)
        def _():
            to_partner(6, 0)
            to_partner(5, 1)

        @pl.when(i == 1)
        def _():
            for j, n in ((6, 0), (5, 1)):
                from_partner(j, n)
                for part in range(4):
                    leave(j, part, cur.at[n], cur_gate.at[n])

        @pl.when(i <= 1)
        def _():
            s = 15 - i
            gradients_of(prob_low, grad_low, ds_all, 14 * 256 + i * 256, [(s, pairs(s))])

            @pl.when(i == 0)
            def _():
                to_partner(7, 0)

            @pl.when(i == 1)
            def _():
                from_partner(7, 0)
                for part in range(4):
                    leave(7, part, cur.at[0], cur_gate.at[0])

        @pl.when(i == 2)
        def _():
            to_partner(2, 0)
            to_partner(4, 1)

        for at, j, mine in ((3, 1, 2), (4, 3, 4), (5, 0, 1), (6, None, 3)):
            @pl.when(i == at)
            def _():
                if j is not None:
                    to_partner(j, 1)
                if at == 5:
                    join(2, (2, 3), (6,))
                from_partner(mine, 0)
                for part in range(4):
                    if (mine, part // 2) in ((1, 1), (3, 0)):
                        leave(mine, part, cur.at[0], cur_gate.at[0])
                held[mine - 1] = cur[0]
                held_gate[mine - 1] = cur_gate[0]
                if at == 4:
                    join(2, (0, 1), (6,))
                if at == 6:
                    own[...] = cur[1]
                    own_gate[...] = cur_gate[1]

        return 0

    def query_pass(ds_all, c, _):
        @pl.when(c == 1)
        def _():
            join(1, (0, 1), (2,))
            join(3, (2, 3), (2,))

        cols = pl.ds(pl.multiple_of(c * 256, 256), 256)
        acc = jnp.dot(wt_all[...], ds_all[:, cols], preferred_element_type=F32) * SCALE
        for q in range(2):
            for h in range(2):
                tile = acc[q * SPAN:(q + 1) * SPAN, h * SPAN:(h + 1) * SPAN].T
                lanes = pl.ds(pl.multiple_of(c * 256 + h * SPAN, SPAN), SPAN)
                dq_ref[q * SPAN:(q + 1) * SPAN, lanes] = tile.astype(BF16)
        return 0

    def second(prob_low, grad_low, ds_all):
        lax.fori_loop(0, 7, functools.partial(second_pass, prob_low, grad_low, ds_all), 0)
        gradients_of(prob_low, grad_low, ds_all, CROSS * 256, [(CROSS, pair_across())])
        own[...] = own[...] + cur[0]
        own_gate[...] = own_gate[...] + cur_gate[0]
        join(4, (0, 1, 2, 3), (5, 7))
        lax.fori_loop(0, 4, functools.partial(query_pass, ds_all), 0)

    pl.run_scoped(second, pltpu.VMEM((512, WIDE), BF16), pltpu.VMEM((512, WIDE), BF16), pltpu.VMEM((PAIRS * SPAN, WIDE), BF16))

    pre_copy(0).wait_recv()
    for part in range(4):
        add(own, own_gate, part, pre_in.at[0])
    for j in (4, 1, 3):
        for part in range(4):
            sum_copy(j, part).wait_recv()
            add(own, own_gate, part, sum_in.at[j - 1])
    dk_ref[...] = own[0:256, :].astype(BF16)
    dv_ref[...] = own[256:512, :].astype(BF16)
    gate_sum = jnp.concatenate([own_gate[0:1, :], own_gate[1:2, :]], axis=1)
    dg_ref[...] = -gate_sum / (1.0 + jnp.exp(-gate_ref[...].astype(F32)))

    for sent, sem in ((blocks.at[pl.ds(0, 15)], block_send), (pre_out, pre_send), (sum_out, sum_send)):
        pltpu.make_async_remote_copy(
            src_ref=sent, dst_ref=sent, send_sem=sem, recv_sem=block_recv.at[0],
            device_id={"ctx": partner}, device_id_type=MESH).wait_send()


def hand_over(*refs):
    copies = [pltpu.make_async_copy(refs[n], refs[4 + n], refs[8].at[n]) for n in range(4)]
    for copy in copies:
        copy.start()
    for copy in copies:
        copy.wait()


def on_device(queries, keys, values, gate_logit, out_grad, stretch_place):
    rows = 2 * SPAN
    vmem = pl.BlockSpec(memory_space=pltpu.VMEM)
    anywhere = pl.BlockSpec(memory_space=pl.ANY)
    dma = pltpu.SemaphoreType.DMA
    outs = (
        jax.ShapeDtypeStruct((rows, WIDE), BF16),
        jax.ShapeDtypeStruct((rows, SPAN), BF16),
        jax.ShapeDtypeStruct((rows, SPAN), BF16),
        jax.ShapeDtypeStruct((1, rows), F32),
    )
    results = pl.pallas_call(
        kernel,
        out_shape=tuple(pltpu.VMEM(out.shape, out.dtype) for out in outs),
        in_specs=[pl.BlockSpec(memory_space=pltpu.SMEM), anywhere, anywhere, anywhere, vmem, anywhere],
        out_specs=(vmem,) * 4,
        scratch_shapes=[
            pltpu.VMEM((2 * CHIPS, ROWS, SPAN), BF16),
            pltpu.VMEM((WIDE, rows), BF16),
            pltpu.VMEM((WIDE, rows), BF16),
            pltpu.VMEM((rows, PAIRS * SPAN), BF16),
            pltpu.VMEM((PAIRS, SPAN, WIDE), F32),
            pltpu.VMEM((PAIRS, SPAN, WIDE), F32),
            pltpu.VMEM((PAIRS, 3, 8, WIDE), F32),
            pltpu.VMEM((6, 8, WIDE), F32),
            pltpu.VMEM((2, 2 * rows, SPAN), F32),
            pltpu.VMEM((2, 8, SPAN), F32),
            pltpu.VMEM((2 * rows, SPAN), F32),
            pltpu.VMEM((8, SPAN), F32),
            pltpu.VMEM((4, 2 * rows, SPAN), F32),
            pltpu.VMEM((4, 8, SPAN), F32),
            pltpu.VMEM((CHIPS, ROWS, SPAN), BF16),
            pltpu.VMEM((CHIPS, ROWS, SPAN), BF16),
            pltpu.VMEM((CHIPS - 1, ROWS, SPAN), BF16),
            pltpu.VMEM((CHIPS - 1, ROWS, SPAN), BF16),
            dma((4,)), dma, dma((25,)), dma, dma((CHIPS,)), dma, dma((CHIPS - 1, 4)),
        ],
        compiler_params=pltpu.CompilerParams(
            collective_id=0, has_side_effects=True, vmem_limit_bytes=63 * 1024 * 1024),
    )(stretch_place, queries, keys, values, gate_logit.T, out_grad)
    dq, dk, dv, dg = pl.pallas_call(
        hand_over,
        out_shape=outs,
        in_specs=[vmem] * 4,
        out_specs=(anywhere,) * 4,
        scratch_shapes=[dma((4,))],
        compiler_params=pltpu.CompilerParams(vmem_limit_bytes=1024 * 1024),
    )(*results)
    return dq, dk, dv, dg.T


def solution(mesh):
    whole = P("ctx", "head")
    return jax.shard_map(
        on_device, mesh=mesh, in_specs=(whole,) * 5 + (P(),), out_specs=(whole,) * 4, check_vma=False)
```
